512 devices in a mesh: feat: 64 (over z, y), tok: 8 (over x, core).
Axes of the slice: x: 4, y: 4, z: 16, core: 2. Of those that a mesh axis runs over, the one named last changes fastest.
Arguments:
- acts: bfloat16 [4096, 2048], P('feat', 'tok')
- dec_bias: float32 [4096], P('feat'), may hold values from -3 to 3
- enc_weight: bfloat16 [4096, 16384], P(None, 'feat')
- enc_bias: float32 [16384], P('feat'), may hold values from -3 to 3
- dec_weight: bfloat16 [16384, 4096], P('feat'), may hold values from -0.046875 to 0.046875
- dead_ids: int32 [64, 256], P('feat'), may hold values from 0 to 255, each once within a row
- tile_count: int32 [64, 8], replicated, may hold values from 0 to 32, as said below
- sample_rows: int32 [64, 8, 32], P(None, 'tok'), may hold values from 0 to 255
Outputs:
- new_enc: bfloat16 [16384, 4096], P(('feat', 'tok'))
- new_dec: bfloat16 [16384, 4096], P(('feat', 'tok'))
- reencoded: bfloat16 [2048, 16384], P('tok', 'feat')
- token_loss: float32 [2048], P('tok')
The draws below stay inside these ranges and needn't reach their ends.
Inputs may be any that keep to these rules, and one draw needn't show every extreme that they name: `tile_count`: in every shard some tile holds fewer than 32 valid slots, and some tile of some shard is full. Each row of dead_ids names every latent of its shard once.
All inputs are finite; a program needn't handle non-finite values.
Results may differ from the reference program's by a relative error of at most 0.0062.
Values may be sent and summed in bfloat16 or wider, within the bound.
No kernel may reach another device: no remote copies, remote signals or barrier semaphores. Data moves between devices by JAX's collectives and lax.ppermute only.
A program may use at most 64 MiB of HBM per device.

```python
import jax
import jax.numpy as jnp
from jax import lax

D = 4096
LAT_DEV = 256
TOK_DEV = 256
LATENTS = 16384
TOKENS = 2048
SLOTS = 256
TILE = 32
N_FEAT = 64
N_TOK = 8


def draw_acts(key, part):
    key = jax.random.fold_in(key, 5)
    keys = jax.random.split(key, 2)
    depth = jnp.arange(D, dtype=jnp.float32) / D
    rough = jnp.exp(jax.random.uniform(keys[1], (D, 1), minval=-0.7, maxval=0.7))
    trend = jnp.exp(jnp.log(3.0) * (depth - 0.5))[:, None]
    noise = jax.random.normal(keys[0], (D, TOKENS))
    return (noise * trend * rough).astype(jnp.bfloat16)


def draw_enc_weight(key, part):
    key = jax.random.fold_in(key, 7)
    keys = jax.random.split(key, 3)
    column = jnp.arange(LATENTS, dtype=jnp.float32) / LATENTS
    spread = jnp.exp(jax.random.uniform(keys[1], (1, LATENTS), minval=jnp.log(0.32), maxval=jnp.log(3.2)))
    rowwise = jnp.exp(jax.random.uniform(keys[2], (D, 1), minval=-0.5, maxval=0.5))
    trend = jnp.exp(jnp.log(3.0) * (column - 0.5))[None, :]
    noise = jax.random.normal(keys[0], (D, LATENTS))
    return (noise * trend * spread * rowwise * D ** (-0.5)).astype(jnp.bfloat16)


def draw_tile_count(key, part):
    key = jax.random.fold_in(key, 11)
    keys = jax.random.split(key, 4)
    level = jax.random.randint(keys[0], (N_FEAT, 1), TILE // 4, TILE + 1)
    jitter = jax.random.randint(keys[1], (N_FEAT, N_TOK), 0, TILE // 4 + 1)
    counts = jnp.maximum(level - jitter, 0)
    capped = jax.random.randint(keys[2], (N_FEAT, 1), 0, N_TOK)
    tile_ids = jnp.arange(N_TOK)[None, :]
    counts = jnp.where(tile_ids == capped, jnp.minimum(counts, TILE - 1), counts)
    chosen = jax.random.randint(keys[3], (), 0, N_FEAT)
    full_tile = (capped[chosen, 0] + 1) % N_TOK
    shard_ids = jnp.arange(N_FEAT)[:, None]
    counts = jnp.where((shard_ids == chosen) & (tile_ids == full_tile), TILE, counts)
    return counts.astype(jnp.int32)


def plant(result, rng, smallest, top_value):
    longest = result.shape.index(max(result.shape))
    spots = []
    for shift in (0, 1):
        where = [jax.random.randint(jax.random.fold_in(rng, axis), (), 0, length) for axis, length in enumerate(result.shape)]
        where[longest] = (where[longest] + shift) % result.shape[longest]
        spots.append(tuple(where))
    return result.at[spots[0]].set(smallest).at[spots[1]].set(top_value)


def shard_levels(stream_key, extent, shards, smallest, top_value):
    level = 1.0
    for axis_at, blocks in shards:
        draws = jax.random.uniform(jax.random.fold_in(jax.random.fold_in(stream_key, 6), axis_at), (blocks,), jnp.float32, smallest / len(shards), top_value / len(shards))
        level = level * jnp.repeat(jnp.exp(draws), extent[axis_at] // blocks).reshape((-1,) + (1,) * (len(extent) - 1 - axis_at))
    return level


def centred(rng, shape, width, limit, shards=(), held_as=jnp.bfloat16):
    level = shard_levels(rng, shape, shards, -0.22, 0.18) if shards else 1.0
    array = jax.random.normal(rng, shape, jnp.float32) * width * level
    return jnp.minimum(jnp.maximum(array, -limit), limit).astype(held_as)


def setup_inputs(seed: int = 0) -> dict:
    splits = jax.random.split(jax.random.key(seed), 9)
    return {
        "acts": draw_acts(jax.random.fold_in(splits[8], 71), 0),
        "dec_bias": centred(splits[1], (D,), 0.5, 3.0, ((0, 64),), jnp.float32),
        "enc_weight": draw_enc_weight(jax.random.fold_in(splits[8], 71), 0),
        "enc_bias": centred(splits[3], (LATENTS,), 0.5, 3.0, ((0, 64),), jnp.float32),
        "dec_weight": centred(splits[4], (LATENTS, D), LATENTS ** -0.5, 0.046875, ((0, 64),)),
        "dead_ids": jax.vmap(lambda own: jax.random.permutation(own, LAT_DEV))(jax.random.split(splits[5], N_FEAT)).reshape((N_FEAT, SLOTS)).astype(jnp.int32),
        "tile_count": draw_tile_count(jax.random.fold_in(splits[8], 71), 0),
        "sample_rows": plant(jax.random.randint(splits[7], (N_FEAT, N_TOK, TILE), 0, TOK_DEV), jax.random.fold_in(splits[7], 1), 0, TOK_DEV - 1).astype(jnp.int32),
    }


ENC_GAIN = 0.2
EPSILON = 1e-06

def reference(acts, dec_bias, enc_weight, enc_bias, dec_weight, dead_ids, tile_count, sample_rows):
    centered = (acts.astype(jnp.float32) - dec_bias.astype(jnp.float32)[:, None]).astype(jnp.bfloat16)
    position = jnp.arange(TILE, dtype=jnp.int32)
    valid = (position[None, None, :] < tile_count[:, :, None]).reshape(N_FEAT, SLOTS)
    latent_ids = jnp.arange(LAT_DEV, dtype=jnp.int32)
    hits = (dead_ids[:, :, None] == latent_ids[None, None, :]) & valid[:, :, None]
    alive = (1.0 - jnp.any(hits, axis=1).astype(jnp.float32)).reshape(LATENTS)
    preact = jnp.dot(centered.T, enc_weight, preferred_element_type=jnp.float32)
    features = (jnp.maximum(preact + enc_bias, 0.0) * alive).astype(jnp.bfloat16)
    recon = jnp.dot(features, dec_weight, preferred_element_type=jnp.float32)
    error = centered.T.astype(jnp.float32) - recon
    token_loss = lax.optimization_barrier(jnp.mean(error * error, axis=1))
    error_b = error.astype(jnp.bfloat16)
    weight_f = enc_weight.astype(jnp.float32)
    norms = jnp.sqrt(lax.optimization_barrier(jnp.sum(weight_f * weight_f, axis=0)))
    alive_total = (N_FEAT * LAT_DEV - jnp.sum(tile_count)).astype(jnp.float32)
    mean_norm = jnp.sum(norms * alive) / alive_total
    offsets = (jnp.arange(N_TOK, dtype=jnp.int32) * TOK_DEV)[None, :, None]
    picked = error_b[(sample_rows + offsets).reshape(-1)]
    picked_f = picked.astype(jnp.float32)
    scale = lax.rsqrt(lax.optimization_barrier(jnp.sum(picked_f * picked_f, axis=1, keepdims=True)) + EPSILON)
    unit = picked_f * scale * valid.reshape(-1, 1).astype(jnp.float32)
    new_dec = unit.astype(jnp.bfloat16)
    new_enc = (ENC_GAIN * mean_norm * unit).astype(jnp.bfloat16)
    product = lax.dot_general(centered, new_enc, (((0,), (1,)), ((), ())), preferred_element_type=jnp.float32)
    reencoded = jnp.maximum(product, 0.0).astype(jnp.bfloat16)
    return (new_enc, new_dec, reencoded, token_loss)
```

```python
import jax
import jax.numpy as jnp
from jax import lax
from jax.experimental import pallas as pl
from jax.experimental.pallas import tpu as pltpu
from jax.sharding import Mesh, PartitionSpec as P

ENC_GAIN = 0.2
EPSILON = 1e-06
F32 = jnp.float32
BF16 = jnp.bfloat16
VM = pl.BlockSpec(memory_space=pltpu.VMEM)
SM = pl.BlockSpec(memory_space=pltpu.SMEM)
EXTRA = 16


def kernel_call(body, out_shape, in_specs, flops, nbytes, scratch=()):
    multi = isinstance(out_shape, (tuple, list))
    return pl.pallas_call(
        body,
        out_shape=out_shape,
        in_specs=in_specs,
        out_specs=[VM] * len(out_shape) if multi else VM,
        scratch_shapes=list(scratch),
        compiler_params=pltpu.CompilerParams(vmem_limit_bytes=24 << 20),
        cost_estimate=pl.CostEstimate(flops=flops, bytes_accessed=nbytes, transcendentals=0),
    )


def split3(v):
    hi = v.astype(BF16)
    rest = v - hi.astype(F32)
    mid = rest.astype(BF16)
    lo = (rest - mid.astype(F32)).astype(BF16)
    return hi, mid, lo


def prepare(enc_ref, dec_ref, alive_ref, rows_ref, enc_t_ref, dec_t_ref, onehot_ref, stat_ref):
    latents = enc_ref.shape[1]
    total = jnp.zeros((1, latents), F32)
    for y in range(4):
        for pair in range(8):
            parts = []
            for z in (2 * pair, 2 * pair + 1):
                block = enc_ref[pl.ds((z * 4 + y) * 64, 64), :]
                wide = block.astype(F32)
                total = total + jnp.sum(wide * wide, axis=0, keepdims=True)
                parts.append(block)
            enc_t_ref[:, pl.ds(y * 1024 + pair * 128, 128)] = jnp.concatenate(parts, 0).T
    stat_ref[...] = jnp.sum(jnp.sqrt(total) * alive_ref[...], axis=1, keepdims=True)
    for block in range(16):
        dec_t_ref[pl.ds(block * 256, 256), :] = dec_ref[:, pl.ds(block * 256, 256)].T
    tokens = onehot_ref.shape[0]
    for block in range(16):
        cols = pl.ds(block * 128, 128)
        token = lax.broadcasted_iota(jnp.int32, (tokens, 128), 0)
        onehot_ref[:, cols] = jnp.where(token == rows_ref[:, cols], 1.0, 0.0).astype(BF16)


def turn(g_ref, out_ref):
    for z in range(16):
        for pair in range(2):
            y = 2 * pair
            both = jnp.concatenate(
                [
                    g_ref[pl.ds((y * 16 + z) * 64, 64), :],
                    g_ref[pl.ds(((y + 1) * 16 + z) * 64, 64), :],
                ],
                0,
            )
            out_ref[:, pl.ds(z * 256 + pair * 128, 128)] = both.T


def forward(enc_t_ref, g_ref, bias_ref, alive_ref, dec_t_ref, out_ref):
    pre = jnp.dot(enc_t_ref[...], g_ref[...], preferred_element_type=F32)
    feat = (jnp.maximum(pre + bias_ref[...], 0.0) * alive_ref[...]).astype(BF16)
    for block in range(16):
        rows = pl.ds(block * 256, 256)
        out_ref[rows, :] = jnp.dot(
            dec_t_ref[rows, :], feat, preferred_element_type=F32
        ).astype(BF16)


def residual(part_ref, own_ref, onehot_ref, stat_ref, out_ref):
    recon = part_ref[0].astype(F32)
    for z in range(1, 16):
        recon = recon + part_ref[z].astype(F32)
    error = own_ref[...].astype(F32) - recon
    loss = jnp.sum(error * error, axis=0, keepdims=True)
    loss = jnp.concatenate([loss[:, :128], loss[:, 128:]], 0)
    stat = jnp.broadcast_to(stat_ref[...], (2, 128))
    pad = jnp.zeros((4, 128), F32)
    pieces = [split3(v) for v in (loss, stat)]
    extra = jnp.concatenate([p.astype(F32) for s in pieces for p in s] + [pad], 0).astype(BF16)
    error_b = error.astype(BF16)
    for z in range(16):
        picked = jnp.dot(
            error_b, onehot_ref[:, pl.ds(z * 128, 128)], preferred_element_type=F32
        )
        out_ref[z, pl.ds(0, 64), :] = picked.astype(BF16)
        out_ref[z, pl.ds(64, EXTRA), :] = extra


def relay(in_ref, out_ref):
    riders = in_ref[0, pl.ds(64, EXTRA), :].astype(F32)
    hi, mid, lo = riders[0:2], riders[2:4], riders[4:6]
    shi, smid, slo = riders[6:8], riders[8:10], riders[10:12]
    loss = hi + mid + lo
    stat = shi + smid + slo
    for z in range(1, 16):
        riders = in_ref[z, pl.ds(64, EXTRA), :].astype(F32)
        loss = loss + (riders[0:2] + riders[2:4] + riders[4:6])
        stat = stat + (riders[6:8] + riders[8:10] + riders[10:12])
    row = jnp.concatenate([loss[0:1], loss[1:2], stat[0:1]], 1)
    row = jnp.concatenate(
        [p.astype(F32) for p in split3(row)] + [jnp.zeros((EXTRA - 3, 384), F32)], 0
    ).astype(BF16)
    row = jnp.concatenate([row, jnp.zeros((EXTRA, 640), BF16)], 1)
    for pair in range(8):
        both = jnp.concatenate(
            [in_ref[2 * pair, pl.ds(0, 64), :], in_ref[2 * pair + 1, pl.ds(0, 64), :]], 0
        ).T
        for y in range(4):
            for x in range(4):
                out_ref[y * 4 + x, pl.ds(0, 32), pl.ds(pair * 128, 128)] = both[
                    y * 32 : y * 32 + 32
                ]
    for block in range(16):
        out_ref[block, pl.ds(32, EXTRA), :] = row


def normalise(place_ref, alive_total_ref, in_ref, all_ref, enc_ref, dec_ref, loss_ref):
    x_own = place_ref[4]
    riders = jnp.zeros((EXTRA, 384), F32)
    for y in range(4):
        riders = riders + in_ref[y * 4 + x_own, pl.ds(32, EXTRA), pl.ds(0, 384)].astype(F32)
    riders = riders[0:1] + riders[1:2] + riders[2:3]
    loss_ref[...] = riders[:, :256] * (1.0 / 4096.0)
    mean_norm = riders[:, 256:257] / alive_total_ref[0]
    gain = ENC_GAIN * mean_norm
    slot = lax.broadcasted_iota(jnp.int32, (32, 1), 0)
    for x in range(4):
        squares = jnp.zeros((32, 1), F32)
        for y in range(4):
            rows = in_ref[y * 4 + x, pl.ds(0, 32), :].astype(F32)
            squares = squares + jnp.sum(rows * rows, axis=1, keepdims=True)
        valid = jnp.where(slot < place_ref[x], 1.0, 0.0)
        scale = lax.rsqrt(squares + EPSILON) * valid
        for y in range(4):
            cols = pl.ds(y * 1024, 1024)
            unit = in_ref[y * 4 + x, pl.ds(0, 32), :].astype(F32) * scale
            row = (gain * unit).astype(BF16)
            all_ref[pl.ds(x * 32, 32), cols] = row

            @pl.when(x == x_own)
            def _(unit=unit, row=row, cols=cols):
                enc_ref[:, cols] = row
                dec_ref[:, cols] = unit.astype(BF16)


def reencode(place_ref, mine_ref, other_ref, tokens_ref, out_ref, rows_ref):
    core = place_ref[5]
    for x in range(4):
        part = pl.ds(x * 32, 32)
        rows_ref[pl.ds(pl.multiple_of(x * 64 + core * 32, 32), 32), :] = mine_ref[part, :]
        rows_ref[pl.ds(pl.multiple_of(x * 64 + 32 - core * 32, 32), 32), :] = other_ref[part, :]
    product = lax.dot_general(
        tokens_ref[...],
        rows_ref[...],
        (((1,), (1,)), ((), ())),
        preferred_element_type=F32,
    )
    out_ref[...] = jnp.maximum(product, 0.0).astype(BF16)


def exchange(value, axes):
    return lax.all_to_all(value, axes, 0, 0, tiled=True)


def on_device(acts, dec_bias, enc_weight, enc_bias, dec_weight, dead_ids, tile_count, sample_rows):
    z_index = lax.axis_index("z")
    y_index = lax.axis_index("y")
    x_index = lax.axis_index("x")
    core_index = lax.axis_index("core")
    feat_index = z_index * 4 + y_index
    width, latents = enc_weight.shape
    tokens = acts.shape[1]
    tile = sample_rows.shape[2]
    slots = dead_ids.shape[1]
    depth = acts.shape[0]

    centered = (acts.astype(F32) - dec_bias[:, None]).astype(BF16)
    by_z = exchange(jnp.broadcast_to(centered[None], (16, depth, tokens)), "z")
    by_z = by_z.reshape(1, 16 * depth, tokens)
    gathered = exchange(jnp.broadcast_to(by_z, (4, 16 * depth, tokens)), "y")
    gathered = gathered.reshape(width, tokens)

    counts = lax.dynamic_index_in_dim(tile_count, feat_index, 0, keepdims=False)
    slot = jnp.arange(slots, dtype=jnp.int32)
    valid = (slot % tile) < jnp.repeat(counts, tile)
    hits = (dead_ids[0][:, None] == jnp.arange(latents, dtype=jnp.int32)[None, :]) & valid[:, None]
    alive = 1.0 - jnp.any(hits, axis=0).astype(F32)
    alive_total = (64 * latents - jnp.sum(tile_count)).astype(F32).reshape(1)

    enc_t, dec_t, onehot, stat = kernel_call(
        prepare,
        (
            jax.ShapeDtypeStruct((latents, width), BF16),
            jax.ShapeDtypeStruct((width, latents), BF16),
            jax.ShapeDtypeStruct((tokens, 64 * tile), BF16),
            jax.ShapeDtypeStruct((1, 1), F32),
        ),
        [VM] * 4,
        1 << 24,
        9 << 20,
    )(enc_weight, dec_weight, alive[None, :], sample_rows.reshape(1, 64 * tile))

    recon = kernel_call(
        forward,
        jax.ShapeDtypeStruct((width, tokens), BF16),
        [VM] * 5,
        4 * width * latents * tokens,
        8 << 20,
    )(enc_t, gathered, enc_bias[:, None], alive[:, None], dec_t)
    by_token = kernel_call(
        turn, jax.ShapeDtypeStruct((tokens, width), BF16), [VM], 1 << 22, 4 << 20
    )(gathered)

    part = exchange(recon.reshape(4, width // 4, tokens), "y")
    part = jnp.sum(part.astype(F32), axis=0).astype(BF16)
    part = exchange(part.reshape(16, depth, tokens), "z")

    source = y_index * 16 + z_index
    own = lax.dynamic_index_in_dim(
        gathered.reshape(64, depth, tokens),
        (source % 4) * 16 + source // 4,
        0,
        keepdims=False,
    )
    picks = kernel_call(
        residual,
        jax.ShapeDtypeStruct((16, depth + EXTRA, 4 * tile), BF16),
        [VM] * 4,
        2 * depth * tokens * 64 * tile,
        2 << 20,
    )(part, own, onehot, stat)
    picks = exchange(picks, "z")
    picks = kernel_call(
        relay,
        jax.ShapeDtypeStruct((16, tile + EXTRA, width // 4), BF16),
        [VM],
        1 << 20,
        2 << 20,
    )(picks)
    picks = exchange(picks, ("y", "x"))

    places = jnp.concatenate(
        [
            lax.dynamic_index_in_dim(counts.reshape(4, 2), core_index, 1, keepdims=False),
            x_index[None],
            core_index[None],
        ]
    ).astype(jnp.int32)
    mine, new_enc, new_dec, token_loss = kernel_call(
        normalise,
        (
            jax.ShapeDtypeStruct((4 * tile, width), BF16),
            jax.ShapeDtypeStruct((tile, width), BF16),
            jax.ShapeDtypeStruct((tile, width), BF16),
            jax.ShapeDtypeStruct((1, tokens), F32),
        ),
        [SM, SM, VM],
        1 << 22,
        3 << 20,
    )(places, alive_total, picks)
    other = lax.ppermute(mine, "core", [(0, 1), (1, 0)])
    reencoded = kernel_call(
        reencode,
        jax.ShapeDtypeStruct((tokens, slots), BF16),
        [SM, VM, VM, VM],
        2 * tokens * slots * width,
        5 << 20,
        [pltpu.VMEM((slots, width), BF16)],
    )(places, mine, other, by_token)
    return (new_enc, new_dec, reencoded, token_loss.reshape(tokens))


def solution(mesh):
    fine = Mesh(mesh.devices.reshape(16, 4, 4, 2), ("z", "y", "x", "core"))
    feat, tok = ("z", "y"), ("x", "core")
    in_specs = (
        P(feat, tok),
        P(feat),
        P(None, feat),
        P(feat),
        P(feat, None),
        P(feat, None),
        P(),
        P(None, tok, None),
    )
    out_specs = (P(feat + tok, None), P(feat + tok, None), P(tok, feat), P(tok))
    return jax.shard_map(
        on_device, mesh=fine, in_specs=in_specs, out_specs=out_specs, check_vma=False
    )
```

```python
import jax
import jax.numpy as jnp
from jax import lax
from jax.experimental import pallas as pl
from jax.experimental.pallas import tpu as pltpu
from jax.sharding import Mesh, PartitionSpec as P

ENC_GAIN = 0.2
EPSILON = 1e-06
F32 = jnp.float32
BF16 = jnp.bfloat16
VM = pl.BlockSpec(memory_space=pltpu.VMEM)
SM = pl.BlockSpec(memory_space=pltpu.SMEM)
EXTRA = 16


def kernel_call(body, out_shape, in_specs, flops, mib, scratch=()):
    multi = isinstance(out_shape, (tuple, list))
    return pl.pallas_call(
        body,
        out_shape=out_shape,
        in_specs=in_specs,
        out_specs=[VM] * len(out_shape) if multi else VM,
        scratch_shapes=list(scratch),
        compiler_params=pltpu.CompilerParams(vmem_limit_bytes=(mib + 4) << 20),
        cost_estimate=pl.CostEstimate(
            flops=flops, bytes_accessed=mib << 20, transcendentals=0
        ),
    )


def split3(v):
    hi = v.astype(BF16)
    rest = v - hi.astype(F32)
    mid = rest.astype(BF16)
    lo = (rest - mid.astype(F32)).astype(BF16)
    return hi, mid, lo


def spread(in_ref, out_ref):
    for y in range(4):
        out_ref[y] = in_ref[...]


def prepare(
    count_ref,
    enc_ref,
    dec_ref,
    bias_ref,
    dead_ref,
    sample_ref,
    enc_t_ref,
    dec_t_ref,
    onehot_ref,
    bias_t_ref,
    alive_ref,
    stat_ref,
):
    latents = enc_ref.shape[1]
    feat = lax.axis_index("z") * 4 + lax.axis_index("y")
    total = jnp.zeros((1, latents), F32)
    for y in range(4):
        for pair in range(8):
            parts = []
            for z in (2 * pair, 2 * pair + 1):
                block = enc_ref[pl.ds((z * 4 + y) * 64, 64), :]
                wide = block.astype(F32)
                total = total + jnp.sum(wide * wide, axis=0, keepdims=True)
                parts.append(block)
            enc_t_ref[:, pl.ds(y * 1024 + pair * 128, 128)] = jnp.concatenate(parts, 0).T
    for block in range(16):
        dec_t_ref[pl.ds(block * 256, 256), :] = dec_ref[:, pl.ds(block * 256, 256)].T

    row = lax.broadcasted_iota(jnp.int32, (latents, latents), 0)
    col = lax.broadcasted_iota(jnp.int32, (latents, latents), 1)
    slot = lax.broadcasted_iota(jnp.int32, (1, latents), 1)
    limit = jnp.zeros((1, latents), jnp.int32)
    for t in range(8):
        limit = jnp.where(slot // 32 == t, count_ref[feat, t], limit)
    dead = jnp.where(slot % 32 < limit, dead_ref[...], -1)
    hit = jnp.where(dead == row, 1.0, 0.0)
    alive = 1.0 - jnp.max(hit, axis=1, keepdims=True)
    alive_ref[...] = alive
    bias_t_ref[...] = jnp.sum(jnp.where(row == col, bias_ref[...], 0.0), axis=1, keepdims=True)
    norms = jnp.sum(jnp.where(row == col, jnp.sqrt(total), 0.0), axis=1, keepdims=True)
    stat_ref[...] = jnp.sum(norms * alive, axis=0, keepdims=True)

    tokens = onehot_ref.shape[0]
    sample = sample_ref[...]
    shard = lax.broadcasted_iota(jnp.int32, sample.shape, 1)
    wide = jnp.concatenate([jnp.where(shard % 4 == y, sample, 0) for y in range(4)], 0)
    wide = jnp.concatenate([wide, jnp.zeros_like(wide)], 1).T
    token = lax.broadcasted_iota(jnp.int32, (tokens, 128), 0)
    for z in range(16):
        wanted = jnp.sum(wide[z * 4 : z * 4 + 4], axis=0, keepdims=True)
        onehot_ref[:, pl.ds(z * 128, 128)] = jnp.where(token == wanted, 1.0, 0.0).astype(BF16)


def fold(in_ref, out_ref):
    for block in range(8):
        rows = pl.ds(block * 128, 128)
        total = in_ref[0, rows, :].astype(F32)
        for y in range(1, 4):
            total = total + in_ref[y, rows, :].astype(F32)
        out_ref[rows, :] = total.astype(BF16)


def turn(g_ref, after_ref, out_ref):
    for z in range(16):
        for pair in range(2):
            y = 2 * pair
            both = jnp.concatenate(
                [
                    g_ref[pl.ds((y * 16 + z) * 64, 64), :],
                    g_ref[pl.ds(((y + 1) * 16 + z) * 64, 64), :],
                ],
                0,
            )
            out_ref[:, pl.ds(z * 256 + pair * 128, 128)] = both.T


def forward(enc_t_ref, g_ref, bias_ref, alive_ref, dec_t_ref, out_ref):
    pre = jnp.dot(enc_t_ref[...], g_ref[...], preferred_element_type=F32)
    feat = (jnp.maximum(pre + bias_ref[...], 0.0) * alive_ref[...]).astype(BF16)
    for block in range(16):
        rows = pl.ds(block * 256, 256)
        out_ref[rows, :] = jnp.dot(
            dec_t_ref[rows, :], feat, preferred_element_type=F32
        ).astype(BF16)


def residual(part_ref, g_ref, onehot_ref, stat_ref, out_ref):
    source = lax.axis_index("y") * 16 + lax.axis_index("z")
    own = g_ref[(source % 4) * 16 + source // 4]
    recon = part_ref[0].astype(F32)
    for z in range(1, 16):
        recon = recon + part_ref[z].astype(F32)
    error = own.astype(F32) - recon
    loss = jnp.sum(error * error, axis=0, keepdims=True)
    loss = jnp.concatenate([loss[:, :128], loss[:, 128:]], 0)
    stat = jnp.broadcast_to(stat_ref[...], (2, 128))
    pad = jnp.zeros((4, 128), F32)
    pieces = [split3(v) for v in (loss, stat)]
    extra = jnp.concatenate([p.astype(F32) for s in pieces for p in s] + [pad], 0).astype(BF16)
    error_b = error.astype(BF16)
    for z in range(16):
        picked = jnp.dot(
            error_b, onehot_ref[:, pl.ds(z * 128, 128)], preferred_element_type=F32
        )
        out_ref[z, pl.ds(0, 64), :] = picked.astype(BF16)
        out_ref[z, pl.ds(64, EXTRA), :] = extra


def relay(in_ref, out_ref):
    riders = in_ref[0, pl.ds(64, EXTRA), :].astype(F32)
    hi, mid, lo = riders[0:2], riders[2:4], riders[4:6]
    shi, smid, slo = riders[6:8], riders[8:10], riders[10:12]
    loss = hi + mid + lo
    stat = shi + smid + slo
    for z in range(1, 16):
        riders = in_ref[z, pl.ds(64, EXTRA), :].astype(F32)
        loss = loss + (riders[0:2] + riders[2:4] + riders[4:6])
        stat = stat + (riders[6:8] + riders[8:10] + riders[10:12])
    row = jnp.concatenate([loss[0:1], loss[1:2], stat[0:1]], 1)
    row = jnp.concatenate(
        [p.astype(F32) for p in split3(row)] + [jnp.zeros((EXTRA - 3, 384), F32)], 0
    ).astype(BF16)
    row = jnp.concatenate([row, jnp.zeros((EXTRA, 640), BF16)], 1)
    for pair in range(8):
        both = jnp.concatenate(
            [in_ref[2 * pair, pl.ds(0, 64), :], in_ref[2 * pair + 1, pl.ds(0, 64), :]], 0
        ).T
        for y in range(4):
            for x in range(4):
                out_ref[y * 4 + x, pl.ds(0, 32), pl.ds(pair * 128, 128)] = both[
                    y * 32 : y * 32 + 32
                ]
    for block in range(16):
        out_ref[block, pl.ds(32, EXTRA), :] = row


def normalise(count_ref, counts_ref, in_ref, all_ref, enc_ref, dec_ref, loss_ref):
    feat = lax.axis_index("z") * 4 + lax.axis_index("y")
    x_own = lax.axis_index("x")
    core = lax.axis_index("core")
    riders = jnp.zeros((EXTRA, 384), F32)
    for y in range(4):
        riders = riders + in_ref[y * 4 + x_own, pl.ds(32, EXTRA), pl.ds(0, 384)].astype(F32)
    riders = riders[0:1] + riders[1:2] + riders[2:3]
    loss_ref[...] = riders[:, :256] * (1.0 / 4096.0)
    dead = jnp.sum(counts_ref[...].astype(F32), axis=0, keepdims=True)
    dead = jnp.sum(dead, axis=1, keepdims=True)
    gain = ENC_GAIN * (riders[:, 256:257] / (16384.0 - dead))
    slot = lax.broadcasted_iota(jnp.int32, (32, 1), 0)
    for x in range(4):
        squares = jnp.zeros((32, 1024), F32)
        for y in range(4):
            rows = in_ref[y * 4 + x, pl.ds(0, 32), :].astype(F32)
            squares = squares + rows * rows
        squares = jnp.sum(squares, axis=1, keepdims=True)
        valid = jnp.where(slot < count_ref[feat, x * 2 + core], 1.0, 0.0)
        scale = lax.rsqrt(squares + EPSILON) * valid
        for y in range(4):
            unit = in_ref[y * 4 + x, pl.ds(0, 32), :].astype(F32) * scale
            all_ref[pl.ds(x * 32, 32), pl.ds(y * 1024, 1024)] = (gain * unit).astype(BF16)

        @pl.when(x == x_own)
        def _(scale=scale, x=x):
            for y in range(4):
                cols = pl.ds(y * 1024, 1024)
                unit = in_ref[y * 4 + x, pl.ds(0, 32), :].astype(F32) * scale
                enc_ref[:, cols] = (gain * unit).astype(BF16)
                dec_ref[:, cols] = unit.astype(BF16)


def reencode(mine_ref, other_ref, tokens_ref, out_ref, rows_ref):
    core = lax.axis_index("core")
    for x in range(4):
        part = pl.ds(x * 32, 32)
        rows_ref[pl.ds(pl.multiple_of(x * 64 + core * 32, 32), 32), :] = mine_ref[part, :]
        rows_ref[pl.ds(pl.multiple_of(x * 64 + 32 - core * 32, 32), 32), :] = other_ref[part, :]
    product = lax.dot_general(
        tokens_ref[...],
        rows_ref[...],
        (((1,), (1,)), ((), ())),
        preferred_element_type=F32,
    )
    out_ref[...] = jnp.maximum(product, 0.0).astype(BF16)


def exchange(value, axes):
    return lax.all_to_all(value, axes, 0, 0, tiled=True)


def shape(*dims, dtype=BF16):
    return jax.ShapeDtypeStruct(dims, dtype)


def on_device(acts, dec_bias, enc_weight, enc_bias, dec_weight, dead_ids, tile_count, sample_rows):
    width, latents = enc_weight.shape
    depth, tokens = acts.shape
    tile = sample_rows.shape[2]
    slots = dead_ids.shape[1]

    centered = (acts.astype(F32) - dec_bias[:, None]).astype(BF16)
    by_z = exchange(jnp.broadcast_to(centered[None], (16, depth, tokens)), "z")
    by_z = by_z.reshape(16 * depth, tokens)
    by_z = kernel_call(spread, shape(4, 16 * depth, tokens), [VM], 1 << 20, 3)(by_z)
    gathered = exchange(by_z, "y").reshape(width, tokens)

    enc_t, dec_t, onehot, bias_t, alive, stat = kernel_call(
        prepare,
        (
            shape(latents, width),
            shape(width, latents),
            shape(tokens, 64 * tile),
            shape(latents, 1, dtype=F32),
            shape(latents, 1, dtype=F32),
            shape(1, 1, dtype=F32),
        ),
        [SM] + [VM] * 5,
        1 << 24,
        9,
    )(
        tile_count,
        enc_weight,
        dec_weight,
        enc_bias.reshape(1, latents),
        dead_ids,
        sample_rows.transpose(1, 2, 0).reshape(tile, 64),
    )

    recon = kernel_call(
        forward, shape(width, tokens), [VM] * 5, 4 * width * latents * tokens, 8
    )(enc_t, gathered, bias_t, alive, dec_t)

    part = exchange(recon.reshape(4, width // 4, tokens), "y")
    part = kernel_call(fold, shape(width // 4, tokens), [VM], 1 << 20, 3)(part)
    part = exchange(part.reshape(16, depth, tokens), "z")

    picks = kernel_call(
        residual,
        shape(16, depth + EXTRA, 4 * tile),
        [VM] * 4,
        2 * depth * tokens * 64 * tile,
        4,
    )(part, gathered.reshape(64, depth, tokens), onehot, stat)
    picks = exchange(picks, "z")
    picks = kernel_call(relay, shape(16, tile + EXTRA, width // 4), [VM], 1 << 20, 2)(picks)
    picks = exchange(picks, ("y", "x"))
    mine, new_enc, new_dec, token_loss = kernel_call(
        normalise,
        (
            shape(4 * tile, width),
            shape(tile, width),
            shape(tile, width),
            shape(1, tokens, dtype=F32),
        ),
        [SM, VM, VM],
        1 << 22,
        4,
    )(tile_count, tile_count, picks)
    by_token = kernel_call(turn, shape(tokens, width), [VM, VM], 1 << 22, 4)(gathered, token_loss)
    other = lax.ppermute(mine, "core", [(0, 1), (1, 0)])
    reencoded = kernel_call(
        reencode,
        shape(tokens, slots),
        [VM, VM, VM],
        2 * tokens * slots * width,
        7,
        [pltpu.VMEM((slots, width), BF16)],
    )(mine, other, by_token)
    return (new_enc, new_dec, reencoded, token_loss.reshape(tokens))


def solution(mesh):
    fine = Mesh(mesh.devices.reshape(16, 4, 4, 2), ("z", "y", "x", "core"))
    feat, tok = ("z", "y"), ("x", "core")
    in_specs = (
        P(feat, tok),
        P(feat),
        P(None, feat),
        P(feat),
        P(feat, None),
        P(feat, None),
        P(),
        P(None, tok, None),
    )
    out_specs = (P(feat + tok, None), P(feat + tok, None), P(tok, feat), P(tok))
    return jax.shard_map(
        on_device, mesh=fine, in_specs=in_specs, out_specs=out_specs, check_vma=False
    )
```

```python
import jax
import jax.numpy as jnp
from jax import lax
from jax.experimental import pallas as pl
from jax.experimental.pallas import tpu as pltpu
from jax.sharding import Mesh, PartitionSpec as P

ENC_GAIN = 0.2
EPSILON = 1e-06
F32 = jnp.float32
BF16 = jnp.bfloat16
VM = pl.BlockSpec(memory_space=pltpu.VMEM)
SM = pl.BlockSpec(memory_space=pltpu.SMEM)
EXTRA = 16


def kernel_call(body, out_shape, in_specs, flops, mib, scratch=(), out_specs=None):
    multi = isinstance(out_shape, (tuple, list))
    if out_specs is None:
        out_specs = [VM] * len(out_shape) if multi else VM
    return pl.pallas_call(
        body,
        out_shape=out_shape,
        in_specs=in_specs,
        out_specs=out_specs,
        scratch_shapes=list(scratch),
        compiler_params=pltpu.CompilerParams(vmem_limit_bytes=(mib + 4) << 20),
        cost_estimate=pl.CostEstimate(
            flops=flops, bytes_accessed=mib << 20, transcendentals=0
        ),
    )


def split3(v):
    hi = v.astype(BF16)
    rest = v - hi.astype(F32)
    mid = rest.astype(BF16)
    lo = (rest - mid.astype(F32)).astype(BF16)
    return hi, mid, lo


def spread(in_ref, out_ref):
    for y in range(4):
        out_ref[y] = in_ref[...]


def forward(count_ref, g_ref, enc_ref, dec_ref, bias_ref, dead_ref, out_ref, t_ref, stat_ref):
    latents = enc_ref.shape[1]
    feat = lax.axis_index("z") * 4 + lax.axis_index("y")
    row = lax.broadcasted_iota(jnp.int32, (latents, latents), 0)
    col = lax.broadcasted_iota(jnp.int32, (latents, latents), 1)
    slot = lax.broadcasted_iota(jnp.int32, (latents, 1), 0)
    limit = jnp.zeros((latents, 1), jnp.int32)
    for t in range(8):
        limit = jnp.where(slot // 32 == t, count_ref[t, feat], limit)
    dead = jnp.sum(jnp.where(row == col, dead_ref[...], 0), axis=1, keepdims=True)
    dead = jnp.where(slot % 32 < limit, dead, -1)
    alive = 1.0 - jnp.max(jnp.where(dead == col, 1.0, 0.0), axis=0, keepdims=True)

    total = jnp.zeros((1, latents), F32)
    pre = bias_ref[...]
    for z in range(16):
        for pair in range(2):
            y = 2 * pair
            both = jnp.concatenate(
                [
                    g_ref[pl.ds((y * 16 + z) * 64, 64), :],
                    g_ref[pl.ds(((y + 1) * 16 + z) * 64, 64), :],
                ],
                0,
            )
            t_ref[:, pl.ds(z * 256 + pair * 128, 128)] = both.T
        rows = enc_ref[pl.ds(z * 256, 256), :]
        wide = rows.astype(F32)
        total = total + jnp.sum(wide * wide, axis=0, keepdims=True)
        pre = pre + jnp.dot(t_ref[:, pl.ds(z * 256, 256)], rows, preferred_element_type=F32)
    stat_ref[...] = jnp.sum(jnp.sqrt(total) * alive, axis=1, keepdims=True)
    feat = (jnp.maximum(pre, 0.0) * alive).astype(BF16)
    for y in range(4):
        for part in range(4):
            out_ref[y, :, pl.ds(part * 256, 256)] = jnp.dot(
                feat,
                dec_ref[:, pl.ds(y * 1024 + part * 256, 256)],
                preferred_element_type=F32,
            ).astype(BF16)


def fold(in_ref, out_ref):
    for block in range(8):
        cols = pl.ds(block * 128, 128)
        total = in_ref[0, :, cols].astype(F32)
        for y in range(1, 4):
            total = total + in_ref[y, :, cols].astype(F32)
        out_ref[cols, :] = total.astype(BF16).T


def residual(part_ref, g_ref, sample_ref, stat_ref, out_ref):
    source = lax.axis_index("y") * 16 + lax.axis_index("z")
    own = g_ref[(source % 4) * 16 + source // 4]
    recon = part_ref[0].astype(F32)
    for z in range(1, 16):
        recon = recon + part_ref[z].astype(F32)
    error = own.astype(F32) - recon
    loss = jnp.sum(error * error, axis=0, keepdims=True)
    loss = jnp.concatenate([loss[:, :128], loss[:, 128:]], 0)
    stat = jnp.broadcast_to(stat_ref[...], (2, 128))
    pad = jnp.zeros((4, 128), F32)
    pieces = [split3(v) for v in (loss, stat)]
    extra = jnp.concatenate([p.astype(F32) for s in pieces for p in s] + [pad], 0).astype(BF16)
    error_b = error.astype(BF16)
    sample = sample_ref[...]
    shard = lax.broadcasted_iota(jnp.int32, sample.shape, 1)
    wide = jnp.concatenate([jnp.where(shard % 4 == y, sample, 0) for y in range(4)], 0)
    wide = jnp.concatenate([wide, jnp.zeros_like(wide)], 1).T
    token = lax.broadcasted_iota(jnp.int32, (error.shape[1], 128), 0)
    for z in range(16):
        wanted = jnp.sum(wide[z * 4 : z * 4 + 4], axis=0, keepdims=True)
        onehot = jnp.where(token == wanted, 1.0, 0.0).astype(BF16)
        picked = jnp.dot(error_b, onehot, preferred_element_type=F32)
        out_ref[z, pl.ds(0, 64), :] = picked.astype(BF16)
        out_ref[z, pl.ds(64, EXTRA), :] = extra


def relay(in_ref, out_ref):
    riders = in_ref[0, pl.ds(64, EXTRA), :].astype(F32)
    hi, mid, lo = riders[0:2], riders[2:4], riders[4:6]
    shi, smid, slo = riders[6:8], riders[8:10], riders[10:12]
    loss = hi + mid + lo
    stat = shi + smid + slo
    for z in range(1, 16):
        riders = in_ref[z, pl.ds(64, EXTRA), :].astype(F32)
        loss = loss + (riders[0:2] + riders[2:4] + riders[4:6])
        stat = stat + (riders[6:8] + riders[8:10] + riders[10:12])
    row = jnp.concatenate([loss[0:1], loss[1:2], stat[0:1]], 1)
    row = jnp.concatenate(
        [p.astype(F32) for p in split3(row)] + [jnp.zeros((EXTRA - 3, 384), F32)], 0
    ).astype(BF16)
    row = jnp.concatenate([row, jnp.zeros((EXTRA, 640), BF16)], 1)
    for pair in range(8):
        both = jnp.concatenate(
            [in_ref[2 * pair, pl.ds(0, 64), :], in_ref[2 * pair + 1, pl.ds(0, 64), :]], 0
        ).T
        for y in range(4):
            for x in range(4):
                out_ref[y * 4 + x, pl.ds(0, 32), pl.ds(pair * 128, 128)] = both[
                    y * 32 : y * 32 + 32
                ]
    for block in range(16):
        out_ref[block, pl.ds(32, EXTRA), :] = row


def tile_scale(in_ref, count, x):
    squares = jnp.zeros((32, 1024), F32)
    for y in range(4):
        rows = in_ref[y * 4 + x, pl.ds(0, 32), :].astype(F32)
        squares = squares + rows * rows
    squares = jnp.sum(squares, axis=1, keepdims=True)
    slot = lax.broadcasted_iota(jnp.int32, (32, 1), 0)
    return lax.rsqrt(squares + EPSILON) * jnp.where(slot < count, 1.0, 0.0)


def read_riders(counts_ref, in_ref, x):
    riders = jnp.zeros((EXTRA, 384), F32)
    for y in range(4):
        riders = riders + in_ref[y * 4 + x, pl.ds(32, EXTRA), pl.ds(0, 384)].astype(F32)
    riders = riders[0:1] + riders[1:2] + riders[2:3]
    dead = jnp.sum(counts_ref[...].astype(F32), axis=0, keepdims=True)
    dead = jnp.sum(dead, axis=1, keepdims=True)
    gain = ENC_GAIN * (riders[:, 256:257] / (16384.0 - dead))
    return riders[:, :256], gain


def normalise(count_ref, counts_ref, in_ref, rows_ref):
    feat = lax.axis_index("z") * 4 + lax.axis_index("y")
    core = lax.axis_index("core")
    _, gain = read_riders(counts_ref, in_ref, 0)
    for x in range(4):
        scale = tile_scale(in_ref, count_ref[x * 2 + core, feat], x)
        for y in range(4):
            unit = in_ref[y * 4 + x, pl.ds(0, 32), :].astype(F32) * scale
            rows_ref[pl.ds(x * 32, 32), pl.ds(y * 1024, 1024)] = (gain * unit).astype(BF16)


def finish(count_ref, counts_ref, in_ref, rows_ref, t_ref, enc_ref, dec_ref, loss_ref, half_ref):
    feat = lax.axis_index("z") * 4 + lax.axis_index("y")
    x_own = lax.axis_index("x")
    core = lax.axis_index("core")
    loss, _ = read_riders(counts_ref, in_ref, x_own)
    loss_ref[...] = loss * (1.0 / 4096.0)
    for x in range(4):

        @pl.when(x == x_own)
        def _(x=x):
            scale = tile_scale(in_ref, count_ref[x * 2 + core, feat], x)
            for y in range(4):
                cols = pl.ds(y * 1024, 1024)
                unit = in_ref[y * 4 + x, pl.ds(0, 32), :].astype(F32) * scale
                dec_ref[:, cols] = unit.astype(BF16)
            enc_ref[...] = rows_ref[pl.ds(x * 32, 32), :]

    half_ref[...] = lax.dot_general(
        t_ref[...], rows_ref[...], (((1,), (1,)), ((), ())), preferred_element_type=F32
    )


def reencode(rows_ref, t_ref, half_ref, out_ref):
    core = lax.axis_index("core")
    other = lax.dot_general(
        t_ref[...], rows_ref[...], (((1,), (1,)), ((), ())), preferred_element_type=F32
    )
    own = half_ref[...]
    first = jnp.where(core == 0, own, other)
    second = jnp.where(core == 0, other, own)
    slots = []
    for x in range(4):
        slots += [first[:, x * 32 : x * 32 + 32], second[:, x * 32 : x * 32 + 32]]
    out_ref[...] = jnp.maximum(jnp.concatenate(slots, 1), 0.0).astype(BF16)


def exchange(value, axes):
    return lax.all_to_all(value, axes, 0, 0, tiled=True)


def shape(*dims, dtype=BF16):
    return jax.ShapeDtypeStruct(dims, dtype)


def on_device(acts, dec_bias, enc_weight, enc_bias, dec_weight, dead_ids, tile_count, sample_rows):
    width, latents = enc_weight.shape
    depth, tokens = acts.shape
    tile = sample_rows.shape[2]
    slots = dead_ids.shape[1]

    counts = tile_count.T
    centered = (acts.astype(F32) - dec_bias[:, None]).astype(BF16)
    by_z = lax.all_gather(centered, "z", axis=0, tiled=True)
    by_z = kernel_call(spread, shape(4, 16 * depth, tokens), [VM], 1 << 20, 3)(by_z)
    gathered = exchange(by_z, "y").reshape(width, tokens)

    recon, by_token, stat = kernel_call(
        forward,
        (shape(4, tokens, width // 4), shape(tokens, width), shape(1, 1, dtype=F32)),
        [SM] + [VM] * 5,
        4 * width * latents * tokens,
        10,
    )(counts, gathered, enc_weight, dec_weight, enc_bias.reshape(1, latents), dead_ids)

    part = exchange(recon, "y")
    part = kernel_call(fold, shape(width // 4, tokens), [VM], 1 << 20, 3)(part)
    part = exchange(part.reshape(16, depth, tokens), "z")

    picks = kernel_call(
        residual,
        shape(16, depth + EXTRA, 4 * tile),
        [VM] * 4,
        2 * depth * tokens * 64 * tile,
        4,
    )(
        part,
        gathered.reshape(64, depth, tokens),
        sample_rows.transpose(1, 2, 0).reshape(tile, 64),
        stat,
    )
    picks = exchange(picks, "z")
    picks = kernel_call(relay, shape(16, tile + EXTRA, width // 4), [VM], 1 << 20, 2)(picks)
    picks = exchange(picks, ("y", "x"))
    rows = kernel_call(normalise, shape(4 * tile, width), [SM, VM, VM], 1 << 21, 3)(
        counts, counts, picks
    )
    other = lax.ppermute(rows, "core", [(0, 1), (1, 0)])
    new_enc, new_dec, token_loss, half = kernel_call(
        finish,
        (
            shape(tile, width),
            shape(tile, width),
            shape(1, tokens, dtype=F32),
            shape(tokens, 4 * tile, dtype=F32),
        ),
        [SM] + [VM] * 4,
        tokens * slots * width,
        6,
    )(counts, counts, picks, rows, by_token)
    reencoded = kernel_call(
        reencode, shape(tokens, slots), [VM] * 3, tokens * slots * width, 4
    )(other, by_token, half)
    return (new_enc, new_dec, reencoded, token_loss.reshape(tokens))


def solution(mesh):
    fine = Mesh(mesh.devices.reshape(16, 4, 4, 2), ("z", "y", "x", "core"))
    feat, tok = ("z", "y"), ("x", "core")
    in_specs = (
        P(feat, tok),
        P(feat),
        P(None, feat),
        P(feat),
        P(feat, None),
        P(feat, None),
        P(),
        P(None, tok, None),
    )
    out_specs = (P(feat + tok, None), P(feat + tok, None), P(tok, feat), P(tok))
    return jax.shard_map(
        on_device, mesh=fine, in_specs=in_specs, out_specs=out_specs, check_vma=False
    )
```

```python
import jax
import jax.numpy as jnp
from jax import lax
from jax.experimental import pallas as pl
from jax.experimental.pallas import tpu as pltpu
from jax.sharding import Mesh, PartitionSpec as P

ENC_GAIN = 0.2
EPSILON = 1e-06
F32 = jnp.float32
BF16 = jnp.bfloat16
VM = pl.BlockSpec(memory_space=pltpu.VMEM)
SM = pl.BlockSpec(memory_space=pltpu.SMEM)
EXTRA = 16


def kernel_call(body, out_shape, in_specs, flops, mib, scratch=(), out_specs=None):
    multi = isinstance(out_shape, (tuple, list))
    if out_specs is None:
        out_specs = [VM] * len(out_shape) if multi else VM
    return pl.pallas_call(
        body,
        out_shape=out_shape,
        in_specs=in_specs,
        out_specs=out_specs,
        scratch_shapes=list(scratch),
        compiler_params=pltpu.CompilerParams(vmem_limit_bytes=(mib + 4) << 20),
        cost_estimate=pl.CostEstimate(
            flops=flops, bytes_accessed=mib << 20, transcendentals=0
        ),
    )


def split3(v):
    hi = v.astype(BF16)
    rest = v - hi.astype(F32)
    mid = rest.astype(BF16)
    lo = (rest - mid.astype(F32)).astype(BF16)
    return hi, mid, lo


def spread(in_ref, out_ref):
    for y in range(4):
        out_ref[y] = in_ref[...]


def forward(count_ref, g_ref, enc_ref, dec_ref, bias_ref, dead_ref, out_ref, t_ref, stat_ref):
    latents = enc_ref.shape[1]
    feat = lax.axis_index("z") * 4 + lax.axis_index("y")
    row = lax.broadcasted_iota(jnp.int32, (latents, latents), 0)
    col = lax.broadcasted_iota(jnp.int32, (latents, latents), 1)
    slot = lax.broadcasted_iota(jnp.int32, (latents, 1), 0)
    limit = jnp.zeros((latents, 1), jnp.int32)
    for t in range(8):
        limit = jnp.where(slot // 32 == t, count_ref[t, feat], limit)
    dead = jnp.sum(jnp.where(row == col, dead_ref[...], 0), axis=1, keepdims=True)
    dead = jnp.where(slot % 32 < limit, dead, -1)
    alive = 1.0 - jnp.max(jnp.where(dead == col, 1.0, 0.0), axis=0, keepdims=True)

    for z in range(16):
        for pair in range(2):
            y = 2 * pair
            both = jnp.concatenate(
                [
                    g_ref[pl.ds((y * 16 + z) * 64, 64), :],
                    g_ref[pl.ds(((y + 1) * 16 + z) * 64, 64), :],
                ],
                0,
            )
            t_ref[:, pl.ds(z * 256 + pair * 128, 128)] = both.T
    pre = jnp.dot(t_ref[...], enc_ref[...], preferred_element_type=F32) + bias_ref[...]
    feat = (jnp.maximum(pre, 0.0) * alive).astype(BF16)
    for y in range(4):
        out_ref[y] = jnp.dot(
            feat, dec_ref[:, pl.ds(y * 1024, 1024)], preferred_element_type=F32
        ).astype(BF16)
    total = jnp.zeros((8, latents), F32)
    for part in range(16):
        wide = enc_ref[pl.ds(part * 256, 256), :].astype(F32)
        total = total + jnp.sum((wide * wide).reshape(32, 8, latents), axis=0)
    norms = jnp.sqrt(jnp.sum(total, axis=0, keepdims=True))
    stat_ref[...] = jnp.sum(norms * alive, axis=1, keepdims=True)


def fold(in_ref, out_ref):
    for block in range(8):
        cols = pl.ds(block * 128, 128)
        total = in_ref[0, :, cols].astype(F32)
        for y in range(1, 4):
            total = total + in_ref[y, :, cols].astype(F32)
        out_ref[cols, :] = total.astype(BF16).T


def residual(part_ref, g_ref, sample_ref, stat_ref, out_ref):
    source = lax.axis_index("y") * 16 + lax.axis_index("z")
    own = g_ref[(source % 4) * 16 + source // 4]
    recon = part_ref[0].astype(F32)
    for z in range(1, 16):
        recon = recon + part_ref[z].astype(F32)
    error = own.astype(F32) - recon
    loss = jnp.sum(error * error, axis=0, keepdims=True)
    loss = jnp.concatenate([loss[:, :128], loss[:, 128:]], 0)
    stat = jnp.broadcast_to(stat_ref[...], (2, 128))
    pad = jnp.zeros((4, 128), F32)
    pieces = [split3(v) for v in (loss, stat)]
    extra = jnp.concatenate([p.astype(F32) for s in pieces for p in s] + [pad], 0).astype(BF16)
    error_b = error.astype(BF16)
    sample = sample_ref[...]
    shard = lax.broadcasted_iota(jnp.int32, sample.shape, 1)
    wide = jnp.concatenate([jnp.where(shard % 4 == y, sample, 0) for y in range(4)], 0)
    wide = jnp.concatenate([wide, jnp.zeros_like(wide)], 1).T
    token = lax.broadcasted_iota(jnp.int32, (error.shape[1], 128), 0)
    for z in range(16):
        wanted = jnp.sum(wide[z * 4 : z * 4 + 4], axis=0, keepdims=True)
        onehot = jnp.where(token == wanted, 1.0, 0.0).astype(BF16)
        picked = jnp.dot(error_b, onehot, preferred_element_type=F32)
        out_ref[z, pl.ds(0, 64), :] = picked.astype(BF16)
        out_ref[z, pl.ds(64, EXTRA), :] = extra


def relay(in_ref, out_ref):
    riders = in_ref[0, pl.ds(64, EXTRA), :].astype(F32)
    hi, mid, lo = riders[0:2], riders[2:4], riders[4:6]
    shi, smid, slo = riders[6:8], riders[8:10], riders[10:12]
    loss = hi + mid + lo
    stat = shi + smid + slo
    for z in range(1, 16):
        riders = in_ref[z, pl.ds(64, EXTRA), :].astype(F32)
        loss = loss + (riders[0:2] + riders[2:4] + riders[4:6])
        stat = stat + (riders[6:8] + riders[8:10] + riders[10:12])
    pieces = [p.astype(F32) for v in (loss, stat) for p in split3(v)]
    riders = jnp.concatenate(pieces + [jnp.zeros((20, 128), F32)], 0).astype(BF16)
    for pair in range(8):
        both = jnp.concatenate(
            [in_ref[2 * pair, pl.ds(0, 64), :], in_ref[2 * pair + 1, pl.ds(0, 64), :]], 0
        ).T
        for y in range(4):
            for x in range(4):
                out_ref[y * 4 + x, :, pl.ds(pair * 128, 128)] = both[y * 32 : y * 32 + 32]
    for block in range(16):
        out_ref[block, :, pl.ds(1024, 128)] = riders


def tile_scale(in_ref, count, x):
    squares = jnp.zeros((32, 1024), F32)
    for y in range(4):
        rows = in_ref[y * 4 + x, :, pl.ds(0, 1024)].astype(F32)
        squares = squares + rows * rows
    squares = jnp.sum(squares, axis=1, keepdims=True)
    slot = lax.broadcasted_iota(jnp.int32, (32, 1), 0)
    return lax.rsqrt(squares + EPSILON) * jnp.where(slot < count, 1.0, 0.0)


def read_riders(counts_ref, in_ref, x):
    riders = jnp.zeros((EXTRA, 128), F32)
    for y in range(4):
        riders = riders + in_ref[y * 4 + x, pl.ds(0, EXTRA), pl.ds(1024, 128)].astype(F32)
    loss = riders[0:2] + riders[2:4] + riders[4:6]
    stat = riders[6:7] + riders[8:9] + riders[10:11]
    dead = jnp.sum(counts_ref[...].astype(F32), axis=0, keepdims=True)
    dead = jnp.sum(dead, axis=1, keepdims=True)
    gain = ENC_GAIN * (stat[:, 0:1] / (16384.0 - dead))
    return jnp.concatenate([loss[0:1], loss[1:2]], 1), gain


def normalise(count_ref, counts_ref, in_ref, rows_ref):
    feat = lax.axis_index("z") * 4 + lax.axis_index("y")
    core = lax.axis_index("core")
    _, gain = read_riders(counts_ref, in_ref, 0)
    for x in range(4):
        scale = tile_scale(in_ref, count_ref[x * 2 + core, feat], x)
        for y in range(4):
            unit = in_ref[y * 4 + x, :, pl.ds(0, 1024)].astype(F32) * scale
            rows_ref[pl.ds(x * 32, 32), pl.ds(y * 1024, 1024)] = (gain * unit).astype(BF16)


def finish(count_ref, counts_ref, in_ref, rows_ref, t_ref, enc_ref, dec_ref, loss_ref, half_ref):
    feat = lax.axis_index("z") * 4 + lax.axis_index("y")
    x_own = lax.axis_index("x")
    core = lax.axis_index("core")
    loss, _ = read_riders(counts_ref, in_ref, x_own)
    loss_ref[...] = loss * (1.0 / 4096.0)
    for x in range(4):

        @pl.when(x == x_own)
        def _(x=x):
            scale = tile_scale(in_ref, count_ref[x * 2 + core, feat], x)
            for y in range(4):
                cols = pl.ds(y * 1024, 1024)
                unit = in_ref[y * 4 + x, :, pl.ds(0, 1024)].astype(F32) * scale
                dec_ref[:, cols] = unit.astype(BF16)
            enc_ref[...] = rows_ref[pl.ds(x * 32, 32), :]

    half_ref[...] = lax.dot_general(
        t_ref[...], rows_ref[...], (((1,), (1,)), ((), ())), preferred_element_type=F32
    )


def reencode(rows_ref, t_ref, half_ref, out_ref):
    core = lax.axis_index("core")
    other = lax.dot_general(
        t_ref[...], rows_ref[...], (((1,), (1,)), ((), ())), preferred_element_type=F32
    )
    own = half_ref[...]
    first = jnp.where(core == 0, own, other)
    second = jnp.where(core == 0, other, own)
    slots = []
    for x in range(4):
        slots += [first[:, x * 32 : x * 32 + 32], second[:, x * 32 : x * 32 + 32]]
    out_ref[...] = jnp.maximum(jnp.concatenate(slots, 1), 0.0).astype(BF16)


def exchange(value, axes):
    return lax.all_to_all(value, axes, 0, 0, tiled=True)


def shape(*dims, dtype=BF16):
    return jax.ShapeDtypeStruct(dims, dtype)


def on_device(acts, dec_bias, enc_weight, enc_bias, dec_weight, dead_ids, tile_count, sample_rows):
    width, latents = enc_weight.shape
    depth, tokens = acts.shape
    tile = sample_rows.shape[2]
    slots = dead_ids.shape[1]

    counts = tile_count.T
    centered = (acts.astype(F32) - dec_bias[:, None]).astype(BF16)
    by_z = lax.all_gather(centered, "z", axis=0, tiled=True)
    by_z = kernel_call(spread, shape(4, 16 * depth, tokens), [VM], 1 << 20, 3)(by_z)
    gathered = exchange(by_z, "y").reshape(width, tokens)

    recon, by_token, stat = kernel_call(
        forward,
        (shape(4, tokens, width // 4), shape(tokens, width), shape(1, 1, dtype=F32)),
        [SM] + [VM] * 5,
        4 * width * latents * tokens,
        10,
    )(counts, gathered, enc_weight, dec_weight, enc_bias.reshape(1, latents), dead_ids)

    part = exchange(recon, "y")
    part = kernel_call(fold, shape(width // 4, tokens), [VM], 1 << 20, 3)(part)
    part = exchange(part.reshape(16, depth, tokens), "z")

    picks = kernel_call(
        residual,
        shape(16, depth + EXTRA, 4 * tile),
        [VM] * 4,
        2 * depth * tokens * 64 * tile,
        4,
    )(
        part,
        gathered.reshape(64, depth, tokens),
        sample_rows.transpose(1, 2, 0).reshape(tile, 64),
        stat,
    )
    picks = exchange(picks, "z")
    picks = kernel_call(relay, shape(16, tile, width // 4 + 128), [VM], 1 << 20, 2)(picks)
    picks = exchange(picks, ("y", "x"))
    rows = kernel_call(normalise, shape(4 * tile, width), [SM, VM, VM], 1 << 21, 3)(
        counts, counts, picks
    )
    other = lax.ppermute(rows, "core", [(0, 1), (1, 0)])
    new_enc, new_dec, token_loss, half = kernel_call(
        finish,
        (
            shape(tile, width),
            shape(tile, width),
            shape(1, tokens, dtype=F32),
            shape(tokens, 4 * tile, dtype=F32),
        ),
        [SM] + [VM] * 4,
        tokens * slots * width,
        6,
    )(counts, counts, picks, rows, by_token)
    reencoded = kernel_call(
        reencode, shape(tokens, slots), [VM] * 3, tokens * slots * width, 4
    )(other, by_token, half)
    return (new_enc, new_dec, reencoded, token_loss.reshape(tokens))


def solution(mesh):
    fine = Mesh(mesh.devices.reshape(16, 4, 4, 2), ("z", "y", "x", "core"))
    feat, tok = ("z", "y"), ("x", "core")
    in_specs = (
        P(feat, tok),
        P(feat),
        P(None, feat),
        P(feat),
        P(feat, None),
        P(feat, None),
        P(),
        P(None, tok, None),
    )
    out_specs = (P(feat + tok, None), P(feat + tok, None), P(tok, feat), P(tok))
    return jax.shard_map(
        on_device, mesh=fine, in_specs=in_specs, out_specs=out_specs, check_vma=False
    )
```

```python
import jax
import jax.numpy as jnp
from jax import lax
from jax.experimental import pallas as pl
from jax.experimental.pallas import tpu as pltpu
from jax.sharding import Mesh, PartitionSpec as P

ENC_GAIN = 0.2
EPSILON = 1e-06
F32 = jnp.float32
BF16 = jnp.bfloat16
VM = pl.BlockSpec(memory_space=pltpu.VMEM)
ANY = pl.BlockSpec(memory_space=pl.ANY)
SM = pl.BlockSpec(memory_space=pltpu.SMEM)
EXTRA = 16


def kernel_call(body, out_shape, in_specs, flops, mib, scratch=(), out_specs=None):
    multi = isinstance(out_shape, (tuple, list))
    if out_specs is None:
        out_specs = [VM] * len(out_shape) if multi else VM
    return pl.pallas_call(
        body,
        out_shape=out_shape,
        in_specs=in_specs,
        out_specs=out_specs,
        scratch_shapes=list(scratch),
        compiler_params=pltpu.CompilerParams(vmem_limit_bytes=(mib + 4) << 20),
        cost_estimate=pl.CostEstimate(
            flops=flops, bytes_accessed=mib << 20, transcendentals=0
        ),
    )


def split3(v):
    hi = v.astype(BF16)
    rest = v - hi.astype(F32)
    mid = rest.astype(BF16)
    lo = (rest - mid.astype(F32)).astype(BF16)
    return hi, mid, lo


def spread(in_ref, after_ref, out_ref):
    for y in range(4):
        out_ref[y] = in_ref[...]


def forward(count_ref, g_ref, enc_ref, bias_ref, dead_ref, out_ref, t_ref, stat_ref):
    latents = enc_ref.shape[1]
    feat = lax.axis_index("z") * 4 + lax.axis_index("y")
    row = lax.broadcasted_iota(jnp.int32, (latents, latents), 0)
    col = lax.broadcasted_iota(jnp.int32, (latents, latents), 1)
    slot = lax.broadcasted_iota(jnp.int32, (latents, 1), 0)
    limit = jnp.zeros((latents, 1), jnp.int32)
    for t in range(8):
        limit = jnp.where(slot // 32 == t, count_ref[t, feat], limit)
    dead = jnp.sum(jnp.where(row == col, dead_ref[...], 0), axis=1, keepdims=True)
    dead = jnp.where(slot % 32 < limit, dead, -1)
    alive = 1.0 - jnp.max(jnp.where(dead == col, 1.0, 0.0), axis=0, keepdims=True)

    for z in range(16):
        for pair in range(2):
            y = 2 * pair
            both = jnp.concatenate(
                [
                    g_ref[pl.ds((y * 16 + z) * 64, 64), :],
                    g_ref[pl.ds(((y + 1) * 16 + z) * 64, 64), :],
                ],
                0,
            )
            t_ref[:, pl.ds(z * 256 + pair * 128, 128)] = both.T
    pre = jnp.dot(t_ref[...], enc_ref[...], preferred_element_type=F32) + bias_ref[...]
    feat = (jnp.maximum(pre, 0.0) * alive).astype(BF16)
    for y in range(4):
        out_ref[y] = feat
    total = jnp.zeros((8, latents), F32)
    for part in range(16):
        wide = enc_ref[pl.ds(part * 256, 256), :].astype(F32)
        total = total + jnp.sum((wide * wide).reshape(32, 8, latents), axis=0)
    norms = jnp.sqrt(jnp.sum(total, axis=0, keepdims=True))
    stat_ref[...] = jnp.sum(norms * alive, axis=1, keepdims=True)


def columns(in_ref, out_ref, held_ref, in_sems, out_sems):
    reads = [
        pltpu.make_async_copy(
            in_ref.at[:, pl.ds(y * 1024, 1024)], held_ref.at[y], in_sems.at[y]
        )
        for y in range(4)
    ]
    writes = [
        pltpu.make_async_copy(held_ref.at[y], out_ref.at[y], out_sems.at[y]) for y in range(4)
    ]
    for y in range(4):
        reads[y].start()
    for y in range(4):
        reads[y].wait()
        writes[y].start()
    for y in range(4):
        writes[y].wait()


def rebuild(feat_ref, dec_ref, out_ref):
    for block in range(4):
        cols = pl.ds(block * 256, 256)
        total = jnp.dot(feat_ref[0], dec_ref[0, :, cols], preferred_element_type=F32)
        for y in range(1, 4):
            total = total + jnp.dot(
                feat_ref[y], dec_ref[y, :, cols], preferred_element_type=F32
            )
        out_ref[cols, :] = total.astype(BF16).T


def residual(part_ref, g_ref, sample_ref, stat_ref, out_ref):
    source = lax.axis_index("y") * 16 + lax.axis_index("z")
    own = g_ref[(source % 4) * 16 + source // 4]
    recon = part_ref[0].astype(F32)
    for z in range(1, 16):
        recon = recon + part_ref[z].astype(F32)
    error = own.astype(F32) - recon
    loss = jnp.sum(error * error, axis=0, keepdims=True)
    loss = jnp.concatenate([loss[:, :128], loss[:, 128:]], 0)
    stat = jnp.broadcast_to(stat_ref[...], (2, 128))
    pad = jnp.zeros((4, 128), F32)
    pieces = [split3(v) for v in (loss, stat)]
    extra = jnp.concatenate([p.astype(F32) for s in pieces for p in s] + [pad], 0).astype(BF16)
    error_b = error.astype(BF16)
    sample = sample_ref[...]
    shard = lax.broadcasted_iota(jnp.int32, sample.shape, 1)
    wide = jnp.concatenate([jnp.where(shard % 4 == y, sample, 0) for y in range(4)], 0)
    wide = jnp.concatenate([wide, jnp.zeros_like(wide)], 1).T
    token = lax.broadcasted_iota(jnp.int32, (error.shape[1], 128), 0)
    for z in range(16):
        wanted = jnp.sum(wide[z * 4 : z * 4 + 4], axis=0, keepdims=True)
        onehot = jnp.where(token == wanted, 1.0, 0.0).astype(BF16)
        picked = jnp.dot(error_b, onehot, preferred_element_type=F32)
        out_ref[z, pl.ds(0, 64), :] = picked.astype(BF16)
        out_ref[z, pl.ds(64, EXTRA), :] = extra


def relay(in_ref, out_ref):
    riders = in_ref[0, pl.ds(64, EXTRA), :].astype(F32)
    hi, mid, lo = riders[0:2], riders[2:4], riders[4:6]
    shi, smid, slo = riders[6:8], riders[8:10], riders[10:12]
    loss = hi + mid + lo
    stat = shi + smid + slo
    for z in range(1, 16):
        riders = in_ref[z, pl.ds(64, EXTRA), :].astype(F32)
        loss = loss + (riders[0:2] + riders[2:4] + riders[4:6])
        stat = stat + (riders[6:8] + riders[8:10] + riders[10:12])
    pieces = [p.astype(F32) for v in (loss, stat) for p in split3(v)]
    riders = jnp.concatenate(pieces + [jnp.zeros((20, 128), F32)], 0).astype(BF16)
    for pair in range(8):
        both = jnp.concatenate(
            [in_ref[2 * pair, pl.ds(0, 64), :], in_ref[2 * pair + 1, pl.ds(0, 64), :]], 0
        ).T
        for y in range(4):
            for x in range(4):
                out_ref[y * 4 + x, :, pl.ds(pair * 128, 128)] = both[y * 32 : y * 32 + 32]
    for block in range(16):
        out_ref[block, :, pl.ds(1024, 128)] = riders


def tile_scale(in_ref, count, x):
    squares = jnp.zeros((32, 1024), F32)
    for y in range(4):
        rows = in_ref[y * 4 + x, :, pl.ds(0, 1024)].astype(F32)
        squares = squares + rows * rows
    squares = jnp.sum(squares, axis=1, keepdims=True)
    slot = lax.broadcasted_iota(jnp.int32, (32, 1), 0)
    return lax.rsqrt(squares + EPSILON) * jnp.where(slot < count, 1.0, 0.0)


def read_riders(counts_ref, in_ref, x):
    riders = jnp.zeros((EXTRA, 128), F32)
    for y in range(4):
        riders = riders + in_ref[y * 4 + x, pl.ds(0, EXTRA), pl.ds(1024, 128)].astype(F32)
    loss = riders[0:2] + riders[2:4] + riders[4:6]
    stat = riders[6:7] + riders[8:9] + riders[10:11]
    dead = jnp.sum(counts_ref[...].astype(F32), axis=0, keepdims=True)
    dead = jnp.sum(dead, axis=1, keepdims=True)
    gain = ENC_GAIN * (stat[:, 0:1] / (16384.0 - dead))
    return jnp.concatenate([loss[0:1], loss[1:2]], 1), gain


def normalise(count_ref, counts_ref, in_ref, rows_ref):
    feat = lax.axis_index("z") * 4 + lax.axis_index("y")
    core = lax.axis_index("core")
    _, gain = read_riders(counts_ref, in_ref, 0)
    for x in range(4):
        scale = tile_scale(in_ref, count_ref[x * 2 + core, feat], x)
        for y in range(4):
            unit = in_ref[y * 4 + x, :, pl.ds(0, 1024)].astype(F32) * scale
            rows_ref[pl.ds(x * 32, 32), pl.ds(y * 1024, 1024)] = (gain * unit).astype(BF16)


def finish(count_ref, counts_ref, in_ref, rows_ref, t_ref, enc_ref, dec_ref, loss_ref, half_ref):
    feat = lax.axis_index("z") * 4 + lax.axis_index("y")
    x_own = lax.axis_index("x")
    core = lax.axis_index("core")
    loss, _ = read_riders(counts_ref, in_ref, x_own)
    loss_ref[...] = loss * (1.0 / 4096.0)
    for x in range(4):

        @pl.when(x == x_own)
        def _(x=x):
            scale = tile_scale(in_ref, count_ref[x * 2 + core, feat], x)
            for y in range(4):
                cols = pl.ds(y * 1024, 1024)
                unit = in_ref[y * 4 + x, :, pl.ds(0, 1024)].astype(F32) * scale
                dec_ref[:, cols] = unit.astype(BF16)
            enc_ref[...] = rows_ref[pl.ds(x * 32, 32), :]

    half_ref[...] = lax.dot_general(
        t_ref[...], rows_ref[...], (((1,), (1,)), ((), ())), preferred_element_type=F32
    )


def reencode(rows_ref, t_ref, half_ref, out_ref):
    core = lax.axis_index("core")
    other = lax.dot_general(
        t_ref[...], rows_ref[...], (((1,), (1,)), ((), ())), preferred_element_type=F32
    )
    own = half_ref[...]
    first = jnp.where(core == 0, own, other)
    second = jnp.where(core == 0, other, own)
    slots = []
    for x in range(4):
        slots += [first[:, x * 32 : x * 32 + 32], second[:, x * 32 : x * 32 + 32]]
    out_ref[...] = jnp.maximum(jnp.concatenate(slots, 1), 0.0).astype(BF16)


def exchange(value, axes):
    return lax.all_to_all(value, axes, 0, 0, tiled=True)


def shape(*dims, dtype=BF16):
    return jax.ShapeDtypeStruct(dims, dtype)


def on_device(acts, dec_bias, enc_weight, enc_bias, dec_weight, dead_ids, tile_count, sample_rows):
    width, latents = enc_weight.shape
    depth, tokens = acts.shape
    tile = sample_rows.shape[2]
    slots = dead_ids.shape[1]

    counts = tile_count.T
    centered = (acts.astype(F32) - dec_bias[:, None]).astype(BF16)
    decoder = kernel_call(
        columns,
        shape(4, latents, width // 4),
        [ANY],
        0,
        56,
        [
            pltpu.VMEM((4, latents, width // 4), BF16),
            pltpu.SemaphoreType.DMA((4,)),
            pltpu.SemaphoreType.DMA((4,)),
        ],
        ANY,
    )(dec_weight)
    decoder = exchange(decoder, "y")
    by_z = lax.all_gather(centered, "z", axis=0, tiled=True)
    by_z = kernel_call(spread, shape(4, 16 * depth, tokens), [VM, ANY], 1 << 20, 3)(
        by_z, decoder
    )
    gathered = exchange(by_z, "y").reshape(width, tokens)

    features, by_token, stat = kernel_call(
        forward,
        (shape(4, tokens, latents), shape(tokens, width), shape(1, 1, dtype=F32)),
        [SM] + [VM] * 4,
        2 * width * latents * tokens,
        8,
    )(counts, gathered, enc_weight, enc_bias.reshape(1, latents), dead_ids)
    features = exchange(features, "y")
    part = kernel_call(
        rebuild, shape(width // 4, tokens), [VM, VM], 2 * width * latents * tokens, 4
    )(features, decoder)
    part = exchange(part.reshape(16, depth, tokens), "z")

    picks = kernel_call(
        residual,
        shape(16, depth + EXTRA, 4 * tile),
        [VM] * 4,
        2 * depth * tokens * 64 * tile,
        4,
    )(
        part,
        gathered.reshape(64, depth, tokens),
        sample_rows.transpose(1, 2, 0).reshape(tile, 64),
        stat,
    )
    picks = exchange(picks, "z")
    picks = kernel_call(relay, shape(16, tile, width // 4 + 128), [VM], 1 << 20, 2)(picks)
    picks = exchange(picks, ("y", "x"))
    rows = kernel_call(normalise, shape(4 * tile, width), [SM, VM, VM], 1 << 21, 3)(
        counts, counts, picks
    )
    other = lax.ppermute(rows, "core", [(0, 1), (1, 0)])
    new_enc, new_dec, token_loss, half = kernel_call(
        finish,
        (
            shape(tile, width),
            shape(tile, width),
            shape(1, tokens, dtype=F32),
            shape(tokens, 4 * tile, dtype=F32),
        ),
        [SM] + [VM] * 4,
        tokens * slots * width,
        6,
    )(counts, counts, picks, rows, by_token)
    reencoded = kernel_call(
        reencode, shape(tokens, slots), [VM] * 3, tokens * slots * width, 4
    )(other, by_token, half)
    return (new_enc, new_dec, reencoded, token_loss.reshape(tokens))


def solution(mesh):
    fine = Mesh(mesh.devices.reshape(16, 4, 4, 2), ("z", "y", "x", "core"))
    feat, tok = ("z", "y"), ("x", "core")
    in_specs = (
        P(feat, tok),
        P(feat),
        P(None, feat),
        P(feat),
        P(feat, None),
        P(feat, None),
        P(),
        P(None, tok, None),
    )
    out_specs = (P(feat + tok, None), P(feat + tok, None), P(tok, feat), P(tok))
    return jax.shard_map(
        on_device, mesh=fine, in_specs=in_specs, out_specs=out_specs, check_vma=False
    )
```

```python
import jax
import jax.numpy as jnp
from jax import lax
from jax.experimental import pallas as pl
from jax.experimental.pallas import tpu as pltpu
from jax.sharding import Mesh, PartitionSpec as P

ENC_GAIN = 0.2
EPSILON = 1e-06
F32 = jnp.float32
BF16 = jnp.bfloat16
VM = pl.BlockSpec(memory_space=pltpu.VMEM)
ANY = pl.BlockSpec(memory_space=pl.ANY)
EXTRA = 16


def kernel_call(body, out_shape, in_specs, flops, mib, scratch=(), out_specs=None):
    multi = isinstance(out_shape, (tuple, list))
    if out_specs is None:
        out_specs = [VM] * len(out_shape) if multi else VM
    return pl.pallas_call(
        body,
        out_shape=out_shape,
        in_specs=in_specs,
        out_specs=out_specs,
        scratch_shapes=list(scratch),
        compiler_params=pltpu.CompilerParams(vmem_limit_bytes=(mib + 4) << 20),
        cost_estimate=pl.CostEstimate(
            flops=flops, bytes_accessed=mib << 20, transcendentals=0
        ),
    )


def split3(v):
    hi = v.astype(BF16)
    rest = v - hi.astype(F32)
    mid = rest.astype(BF16)
    lo = (rest - mid.astype(F32)).astype(BF16)
    return hi, mid, lo


def spread(in_ref, after_ref, out_ref):
    for y in range(4):
        out_ref[y] = in_ref[...]


def own_counts(counts_ref):
    counts = counts_ref[...]
    feat = lax.axis_index("z") * 4 + lax.axis_index("y")
    shard = lax.broadcasted_iota(jnp.int32, counts.shape, 1)
    return jnp.sum(jnp.where(shard == feat, counts, 0), axis=1, keepdims=True)


def forward(counts_ref, g_ref, enc_ref, bias_ref, dead_ref, out_ref, t_ref, stat_ref):
    latents = enc_ref.shape[1]
    count = own_counts(counts_ref)
    row = lax.broadcasted_iota(jnp.int32, (latents, latents), 0)
    col = lax.broadcasted_iota(jnp.int32, (latents, latents), 1)
    slot = lax.broadcasted_iota(jnp.int32, (latents, 1), 0)
    limit = jnp.zeros((latents, 1), jnp.int32)
    for t in range(8):
        limit = jnp.where(slot // 32 == t, count[t : t + 1], limit)
    dead = jnp.sum(jnp.where(row == col, dead_ref[...], 0), axis=1, keepdims=True)
    dead = jnp.where(slot % 32 < limit, dead, -1)
    alive = 1.0 - jnp.max(jnp.where(dead == col, 1.0, 0.0), axis=0, keepdims=True)

    for z in range(16):
        for pair in range(2):
            y = 2 * pair
            both = jnp.concatenate(
                [
                    g_ref[pl.ds((y * 16 + z) * 64, 64), :],
                    g_ref[pl.ds(((y + 1) * 16 + z) * 64, 64), :],
                ],
                0,
            )
            t_ref[:, pl.ds(z * 256 + pair * 128, 128)] = both.T
    pre = jnp.dot(t_ref[...], enc_ref[...], preferred_element_type=F32) + bias_ref[...]
    feat = (jnp.maximum(pre, 0.0) * alive).astype(BF16)
    for y in range(4):
        out_ref[y] = feat
    total = jnp.zeros((8, latents), F32)
    for part in range(16):
        wide = enc_ref[pl.ds(part * 256, 256), :].astype(F32)
        total = total + jnp.sum((wide * wide).reshape(32, 8, latents), axis=0)
    norms = jnp.sqrt(jnp.sum(total, axis=0, keepdims=True))
    stat = jnp.sum(norms * alive, axis=1, keepdims=True)
    stat_ref[...] = jnp.broadcast_to(stat, stat_ref.shape)


def columns(in_ref, out_ref, held_ref, in_sems, out_sems):
    reads = [
        pltpu.make_async_copy(
            in_ref.at[:, pl.ds(y * 1024, 1024)], held_ref.at[y], in_sems.at[y]
        )
        for y in range(4)
    ]
    writes = [
        pltpu.make_async_copy(held_ref.at[y], out_ref.at[y], out_sems.at[y]) for y in range(4)
    ]
    for y in range(4):
        reads[y].start()
    for y in range(4):
        reads[y].wait()
        writes[y].start()
    for y in range(4):
        writes[y].wait()


def rebuild(feat_ref, dec_ref, out_ref):
    for block in range(4):
        cols = pl.ds(block * 256, 256)
        total = jnp.dot(feat_ref[0], dec_ref[0, :, cols], preferred_element_type=F32)
        for y in range(1, 4):
            total = total + jnp.dot(
                feat_ref[y], dec_ref[y, :, cols], preferred_element_type=F32
            )
        out_ref[cols, :] = total.astype(BF16).T


def residual(part_ref, g_ref, sample_ref, stat_ref, out_ref):
    source = lax.axis_index("y") * 16 + lax.axis_index("z")
    own = g_ref[(source % 4) * 16 + source // 4]
    recon = part_ref[0].astype(F32)
    for z in range(1, 16):
        recon = recon + part_ref[z].astype(F32)
    error = own.astype(F32) - recon
    loss = jnp.sum(error * error, axis=0, keepdims=True)
    loss = jnp.concatenate([loss[:, :128], loss[:, 128:]], 0)
    stat = stat_ref[pl.ds(0, 2), :]
    pad = jnp.zeros((4, 128), F32)
    pieces = [split3(v) for v in (loss, stat)]
    extra = jnp.concatenate([p.astype(F32) for s in pieces for p in s] + [pad], 0).astype(BF16)
    error_b = error.astype(BF16)
    sample = sample_ref[...]
    shard = lax.broadcasted_iota(jnp.int32, sample.shape, 1)
    wide = jnp.concatenate([jnp.where(shard % 4 == y, sample, 0) for y in range(4)], 0)
    wide = jnp.concatenate([wide, jnp.zeros_like(wide)], 1).T
    token = lax.broadcasted_iota(jnp.int32, (error.shape[1], 128), 0)
    for z in range(16):
        wanted = jnp.sum(wide[z * 4 : z * 4 + 4], axis=0, keepdims=True)
        onehot = jnp.where(token == wanted, 1.0, 0.0).astype(BF16)
        picked = jnp.dot(error_b, onehot, preferred_element_type=F32)
        out_ref[z, pl.ds(0, 64), :] = picked.astype(BF16)
        out_ref[z, pl.ds(64, EXTRA), :] = extra


def relay(in_ref, out_ref):
    riders = in_ref[0, pl.ds(64, EXTRA), :].astype(F32)
    hi, mid, lo = riders[0:2], riders[2:4], riders[4:6]
    shi, smid, slo = riders[6:8], riders[8:10], riders[10:12]
    loss = hi + mid + lo
    stat = shi + smid + slo
    for z in range(1, 16):
        riders = in_ref[z, pl.ds(64, EXTRA), :].astype(F32)
        loss = loss + (riders[0:2] + riders[2:4] + riders[4:6])
        stat = stat + (riders[6:8] + riders[8:10] + riders[10:12])
    pieces = [p.astype(F32) for v in (loss, stat) for p in split3(v)]
    riders = jnp.concatenate(pieces + [jnp.zeros((20, 128), F32)], 0).astype(BF16)
    for pair in range(8):
        both = jnp.concatenate(
            [in_ref[2 * pair, pl.ds(0, 64), :], in_ref[2 * pair + 1, pl.ds(0, 64), :]], 0
        ).T
        for y in range(4):
            for x in range(4):
                out_ref[y * 4 + x, :, pl.ds(pair * 128, 128)] = both[y * 32 : y * 32 + 32]
    for block in range(16):
        out_ref[block, :, pl.ds(1024, 128)] = riders


def tile_scale(in_ref, count, x):
    squares = jnp.zeros((32, 1024), F32)
    for y in range(4):
        rows = in_ref[y * 4 + x, :, pl.ds(0, 1024)].astype(F32)
        squares = squares + rows * rows
    squares = jnp.sum(squares, axis=1, keepdims=True)
    slot = lax.broadcasted_iota(jnp.int32, (32, 1), 0)
    return lax.rsqrt(squares + EPSILON) * jnp.where(slot < count, 1.0, 0.0)


def read_riders(counts_ref, in_ref, x):
    riders = jnp.zeros((EXTRA, 128), F32)
    for y in range(4):
        riders = riders + in_ref[y * 4 + x, pl.ds(0, EXTRA), pl.ds(1024, 128)].astype(F32)
    loss = riders[0:2] + riders[2:4] + riders[4:6]
    stat = riders[6:7] + riders[8:9] + riders[10:11]
    dead = jnp.sum(counts_ref[...].astype(F32), axis=0, keepdims=True)
    dead = jnp.sum(dead, axis=1, keepdims=True)
    gain = ENC_GAIN * (stat[:, 0:1] / (16384.0 - dead))
    return jnp.concatenate([loss[0:1], loss[1:2]], 1), gain


def tile_count(count, t):
    tile = lax.broadcasted_iota(jnp.int32, count.shape, 0)
    return jnp.sum(jnp.where(tile == t, count, 0), axis=0, keepdims=True)


def normalise(counts_ref, in_ref, rows_ref):
    core = lax.axis_index("core")
    count = own_counts(counts_ref)
    _, gain = read_riders(counts_ref, in_ref, 0)
    for x in range(4):
        scale = tile_scale(in_ref, tile_count(count, x * 2 + core), x)
        for y in range(4):
            unit = in_ref[y * 4 + x, :, pl.ds(0, 1024)].astype(F32) * scale
            rows_ref[pl.ds(x * 32, 32), pl.ds(y * 1024, 1024)] = (gain * unit).astype(BF16)


def finish(counts_ref, in_ref, rows_ref, t_ref, enc_ref, dec_ref, loss_ref, half_ref):
    x_own = lax.axis_index("x")
    core = lax.axis_index("core")
    count = own_counts(counts_ref)
    loss, _ = read_riders(counts_ref, in_ref, x_own)
    loss_ref[...] = loss * (1.0 / 4096.0)
    for x in range(4):

        @pl.when(x == x_own)
        def _(x=x):
            scale = tile_scale(in_ref, tile_count(count, x * 2 + core), x)
            for y in range(4):
                cols = pl.ds(y * 1024, 1024)
                unit = in_ref[y * 4 + x, :, pl.ds(0, 1024)].astype(F32) * scale
                dec_ref[:, cols] = unit.astype(BF16)
            enc_ref[...] = rows_ref[pl.ds(x * 32, 32), :]

    half_ref[...] = lax.dot_general(
        t_ref[...], rows_ref[...], (((1,), (1,)), ((), ())), preferred_element_type=F32
    )


def reencode(rows_ref, t_ref, half_ref, out_ref):
    core = lax.axis_index("core")
    other = lax.dot_general(
        t_ref[...], rows_ref[...], (((1,), (1,)), ((), ())), preferred_element_type=F32
    )
    own = half_ref[...]
    first = jnp.where(core == 0, own, other)
    second = jnp.where(core == 0, other, own)
    slots = []
    for x in range(4):
        slots += [first[:, x * 32 : x * 32 + 32], second[:, x * 32 : x * 32 + 32]]
    out_ref[...] = jnp.maximum(jnp.concatenate(slots, 1), 0.0).astype(BF16)


def exchange(value, axes):
    return lax.all_to_all(value, axes, 0, 0, tiled=True)


def shape(*dims, dtype=BF16):
    return jax.ShapeDtypeStruct(dims, dtype)


def on_device(acts, dec_bias, enc_weight, enc_bias, dec_weight, dead_ids, tile_count, sample_rows):
    width, latents = enc_weight.shape
    depth, tokens = acts.shape
    tile = sample_rows.shape[2]
    slots = dead_ids.shape[1]

    counts = tile_count.T
    centered = (acts.astype(F32) - dec_bias[:, None]).astype(BF16)
    decoder = kernel_call(
        columns,
        shape(4, latents, width // 4),
        [ANY],
        0,
        56,
        [
            pltpu.VMEM((4, latents, width // 4), BF16),
            pltpu.SemaphoreType.DMA((4,)),
            pltpu.SemaphoreType.DMA((4,)),
        ],
        ANY,
    )(dec_weight)
    decoder = exchange(decoder, "y")
    by_z = lax.all_gather(centered, "z", axis=0, tiled=True)
    by_z = kernel_call(spread, shape(4, 16 * depth, tokens), [VM, ANY], 1 << 20, 3)(
        by_z, decoder
    )
    gathered = exchange(by_z, "y").reshape(width, tokens)

    features, by_token, stat = kernel_call(
        forward,
        (shape(4, tokens, latents), shape(tokens, width), shape(8, 128, dtype=F32)),
        [VM] * 5,
        2 * width * latents * tokens,
        8,
    )(counts, gathered, enc_weight, enc_bias.reshape(1, latents), dead_ids)
    features = exchange(features, "y")
    part = kernel_call(
        rebuild, shape(width // 4, tokens), [VM, VM], 2 * width * latents * tokens, 4
    )(features, decoder)
    part = exchange(part.reshape(16, depth, tokens), "z")

    picks = kernel_call(
        residual,
        shape(16, depth + EXTRA, 4 * tile),
        [VM] * 4,
        2 * depth * tokens * 64 * tile,
        4,
    )(
        part,
        gathered.reshape(64, depth, tokens),
        sample_rows.transpose(1, 2, 0).reshape(tile, 64),
        stat,
    )
    picks = exchange(picks, "z")
    picks = kernel_call(relay, shape(16, tile, width // 4 + 128), [VM], 1 << 20, 2)(picks)
    picks = exchange(picks, ("y", "x"))
    rows = kernel_call(normalise, shape(4 * tile, width), [VM, VM], 1 << 21, 3)(counts, picks)
    other = lax.ppermute(rows, "core", [(0, 1), (1, 0)])
    new_enc, new_dec, token_loss, half = kernel_call(
        finish,
        (
            shape(tile, width),
            shape(tile, width),
            shape(1, tokens, dtype=F32),
            shape(tokens, 4 * tile, dtype=F32),
        ),
        [VM] * 4,
        tokens * slots * width,
        6,
    )(counts, picks, rows, by_token)
    reencoded = kernel_call(
        reencode, shape(tokens, slots), [VM] * 3, tokens * slots * width, 4
    )(other, by_token, half)
    return (new_enc, new_dec, reencoded, token_loss.reshape(tokens))


def solution(mesh):
    fine = Mesh(mesh.devices.reshape(16, 4, 4, 2), ("z", "y", "x", "core"))
    feat, tok = ("z", "y"), ("x", "core")
    in_specs = (
        P(feat, tok),
        P(feat),
        P(None, feat),
        P(feat),
        P(feat, None),
        P(feat, None),
        P(),
        P(None, tok, None),
    )
    out_specs = (P(feat + tok, None), P(feat + tok, None), P(tok, feat), P(tok))
    return jax.shard_map(
        on_device, mesh=fine, in_specs=in_specs, out_specs=out_specs, check_vma=False
    )
```

```python
import jax
import jax.numpy as jnp
from jax import lax
from jax.experimental import pallas as pl
from jax.experimental.pallas import tpu as pltpu
from jax.sharding import Mesh, PartitionSpec as P

ENC_GAIN = 0.2
EPSILON = 1e-06
F32 = jnp.float32
BF16 = jnp.bfloat16
VM = pl.BlockSpec(memory_space=pltpu.VMEM)
ANY = pl.BlockSpec(memory_space=pl.ANY)
EXTRA = 16


def kernel_call(body, out_shape, in_specs, flops, mib, scratch=(), out_specs=None):
    multi = isinstance(out_shape, (tuple, list))
    if out_specs is None:
        out_specs = [VM] * len(out_shape) if multi else VM
    return pl.pallas_call(
        body,
        out_shape=out_shape,
        in_specs=in_specs,
        out_specs=out_specs,
        scratch_shapes=list(scratch),
        compiler_params=pltpu.CompilerParams(vmem_limit_bytes=(mib + 4) << 20),
        cost_estimate=pl.CostEstimate(
            flops=flops, bytes_accessed=mib << 20, transcendentals=0
        ),
    )


def split3(v):
    hi = v.astype(BF16)
    rest = v - hi.astype(F32)
    mid = rest.astype(BF16)
    lo = (rest - mid.astype(F32)).astype(BF16)
    return hi, mid, lo


def spread(in_ref, after_ref, out_ref):
    for y in range(4):
        out_ref[y] = in_ref[...]


def own_counts(counts_ref):
    counts = counts_ref[...]
    feat = lax.axis_index("z") * 4 + lax.axis_index("y")
    shard = lax.broadcasted_iota(jnp.int32, counts.shape, 1)
    return jnp.sum(jnp.where(shard == feat, counts, 0), axis=1, keepdims=True)


def forward(counts_ref, g_ref, enc_ref, bias_ref, dead_ref, out_ref, t_ref, stat_ref):
    latents = enc_ref.shape[1]
    count = own_counts(counts_ref)
    row = lax.broadcasted_iota(jnp.int32, (latents, latents), 0)
    col = lax.broadcasted_iota(jnp.int32, (latents, latents), 1)
    slot = lax.broadcasted_iota(jnp.int32, (latents, 1), 0)
    limit = jnp.zeros((latents, 1), jnp.int32)
    for t in range(8):
        limit = jnp.where(slot // 32 == t, count[t : t + 1], limit)
    dead = jnp.sum(jnp.where(row == col, dead_ref[...], 0), axis=1, keepdims=True)
    dead = jnp.where(slot % 32 < limit, dead, -1)
    alive = 1.0 - jnp.max(jnp.where(dead == col, 1.0, 0.0), axis=0, keepdims=True)

    for z in range(16):
        for pair in range(2):
            y = 2 * pair
            both = jnp.concatenate(
                [
                    g_ref[pl.ds((y * 16 + z) * 64, 64), :],
                    g_ref[pl.ds(((y + 1) * 16 + z) * 64, 64), :],
                ],
                0,
            )
            t_ref[:, pl.ds(z * 256 + pair * 128, 128)] = both.T
    pre = jnp.dot(t_ref[...], enc_ref[...], preferred_element_type=F32) + bias_ref[...]
    feat = (jnp.maximum(pre, 0.0) * alive).astype(BF16)
    for y in range(4):
        out_ref[y] = feat
    total = jnp.zeros((8, latents), F32)
    for part in range(16):
        wide = enc_ref[pl.ds(part * 256, 256), :].astype(F32)
        total = total + jnp.sum((wide * wide).reshape(32, 8, latents), axis=0)
    norms = jnp.sqrt(jnp.sum(total, axis=0, keepdims=True))
    stat = jnp.sum(norms * alive, axis=1, keepdims=True)
    stat_ref[...] = jnp.broadcast_to(stat, stat_ref.shape)


def columns(in_ref, out_ref, held_ref, in_sems, out_sems):
    own = lax.axis_index("y")
    reads, writes = [], []
    for k in range(1, 4):
        y = lax.rem(own + k, 4)
        cols = pl.ds(pl.multiple_of(y * 1024, 1024), 1024)
        reads.append(
            pltpu.make_async_copy(in_ref.at[:, cols], held_ref.at[k - 1], in_sems.at[k - 1])
        )
        writes.append(
            pltpu.make_async_copy(held_ref.at[k - 1], out_ref.at[y], out_sems.at[k - 1])
        )
    for read in reads:
        read.start()
    for read, write in zip(reads, writes):
        read.wait()
        write.start()
    for write in writes:
        write.wait()


def rebuild(feat_ref, dec_ref, own_ref, out_ref):
    own = lax.axis_index("y")
    for block in range(4):
        cols = pl.ds(block * 256, 256)
        mine = pl.ds(pl.multiple_of(own * 1024 + block * 256, 256), 256)
        total = jnp.dot(feat_ref[own], own_ref[:, mine], preferred_element_type=F32)
        for k in range(1, 4):
            y = lax.rem(own + k, 4)
            total = total + jnp.dot(
                feat_ref[y], dec_ref[y, :, cols], preferred_element_type=F32
            )
        out_ref[cols, :] = total.astype(BF16).T


def residual(part_ref, g_ref, sample_ref, stat_ref, out_ref):
    source = lax.axis_index("y") * 16 + lax.axis_index("z")
    own = g_ref[(source % 4) * 16 + source // 4]
    recon = part_ref[0].astype(F32)
    for z in range(1, 16):
        recon = recon + part_ref[z].astype(F32)
    error = own.astype(F32) - recon
    loss = jnp.sum(error * error, axis=0, keepdims=True)
    loss = jnp.concatenate([loss[:, :128], loss[:, 128:]], 0)
    stat = stat_ref[pl.ds(0, 2), :]
    pad = jnp.zeros((4, 128), F32)
    pieces = [split3(v) for v in (loss, stat)]
    extra = jnp.concatenate([p.astype(F32) for s in pieces for p in s] + [pad], 0).astype(BF16)
    error_b = error.astype(BF16)
    sample = sample_ref[...]
    shard = lax.broadcasted_iota(jnp.int32, sample.shape, 1)
    wide = jnp.concatenate([jnp.where(shard % 4 == y, sample, 0) for y in range(4)], 0)
    wide = jnp.concatenate([wide, jnp.zeros_like(wide)], 1).T
    token = lax.broadcasted_iota(jnp.int32, (error.shape[1], 128), 0)
    for z in range(16):
        wanted = jnp.sum(wide[z * 4 : z * 4 + 4], axis=0, keepdims=True)
        onehot = jnp.where(token == wanted, 1.0, 0.0).astype(BF16)
        picked = jnp.dot(error_b, onehot, preferred_element_type=F32)
        out_ref[z, pl.ds(0, 64), :] = picked.astype(BF16)
        out_ref[z, pl.ds(64, EXTRA), :] = extra


def relay(in_ref, out_ref):
    riders = in_ref[0, pl.ds(64, EXTRA), :].astype(F32)
    hi, mid, lo = riders[0:2], riders[2:4], riders[4:6]
    shi, smid, slo = riders[6:8], riders[8:10], riders[10:12]
    loss = hi + mid + lo
    stat = shi + smid + slo
    for z in range(1, 16):
        riders = in_ref[z, pl.ds(64, EXTRA), :].astype(F32)
        loss = loss + (riders[0:2] + riders[2:4] + riders[4:6])
        stat = stat + (riders[6:8] + riders[8:10] + riders[10:12])
    pieces = [p.astype(F32) for v in (loss, stat) for p in split3(v)]
    riders = jnp.concatenate(pieces + [jnp.zeros((20, 128), F32)], 0).astype(BF16)
    for pair in range(8):
        both = jnp.concatenate(
            [in_ref[2 * pair, pl.ds(0, 64), :], in_ref[2 * pair + 1, pl.ds(0, 64), :]], 0
        ).T
        for y in range(4):
            for x in range(4):
                out_ref[y * 4 + x, :, pl.ds(pair * 128, 128)] = both[y * 32 : y * 32 + 32]
    for block in range(16):
        out_ref[block, :, pl.ds(1024, 128)] = riders


def tile_scale(in_ref, count, x):
    squares = jnp.zeros((32, 1024), F32)
    for y in range(4):
        rows = in_ref[y * 4 + x, :, pl.ds(0, 1024)].astype(F32)
        squares = squares + rows * rows
    squares = jnp.sum(squares, axis=1, keepdims=True)
    slot = lax.broadcasted_iota(jnp.int32, (32, 1), 0)
    return lax.rsqrt(squares + EPSILON) * jnp.where(slot < count, 1.0, 0.0)


def read_riders(counts_ref, in_ref, x):
    riders = jnp.zeros((EXTRA, 128), F32)
    for y in range(4):
        riders = riders + in_ref[y * 4 + x, pl.ds(0, EXTRA), pl.ds(1024, 128)].astype(F32)
    loss = riders[0:2] + riders[2:4] + riders[4:6]
    stat = riders[6:7] + riders[8:9] + riders[10:11]
    dead = jnp.sum(counts_ref[...].astype(F32), axis=0, keepdims=True)
    dead = jnp.sum(dead, axis=1, keepdims=True)
    gain = ENC_GAIN * (stat[:, 0:1] / (16384.0 - dead))
    return jnp.concatenate([loss[0:1], loss[1:2]], 1), gain


def tile_count(count, t):
    tile = lax.broadcasted_iota(jnp.int32, count.shape, 0)
    return jnp.sum(jnp.where(tile == t, count, 0), axis=0, keepdims=True)


def normalise(counts_ref, in_ref, rows_ref):
    core = lax.axis_index("core")
    count = own_counts(counts_ref)
    _, gain = read_riders(counts_ref, in_ref, 0)
    for x in range(4):
        scale = tile_scale(in_ref, tile_count(count, x * 2 + core), x)
        for y in range(4):
            unit = in_ref[y * 4 + x, :, pl.ds(0, 1024)].astype(F32) * scale
            rows_ref[pl.ds(x * 32, 32), pl.ds(y * 1024, 1024)] = (gain * unit).astype(BF16)


def finish(counts_ref, in_ref, rows_ref, t_ref, enc_ref, dec_ref, loss_ref, half_ref):
    x_own = lax.axis_index("x")
    core = lax.axis_index("core")
    count = own_counts(counts_ref)
    loss, _ = read_riders(counts_ref, in_ref, x_own)
    loss_ref[...] = loss * (1.0 / 4096.0)
    for x in range(4):

        @pl.when(x == x_own)
        def _(x=x):
            scale = tile_scale(in_ref, tile_count(count, x * 2 + core), x)
            for y in range(4):
                cols = pl.ds(y * 1024, 1024)
                unit = in_ref[y * 4 + x, :, pl.ds(0, 1024)].astype(F32) * scale
                dec_ref[:, cols] = unit.astype(BF16)
            enc_ref[...] = rows_ref[pl.ds(x * 32, 32), :]

    half_ref[...] = lax.dot_general(
        t_ref[...], rows_ref[...], (((1,), (1,)), ((), ())), preferred_element_type=F32
    )


def reencode(rows_ref, t_ref, half_ref, out_ref):
    core = lax.axis_index("core")
    other = lax.dot_general(
        t_ref[...], rows_ref[...], (((1,), (1,)), ((), ())), preferred_element_type=F32
    )
    own = half_ref[...]
    first = jnp.where(core == 0, own, other)
    second = jnp.where(core == 0, other, own)
    slots = []
    for x in range(4):
        slots += [first[:, x * 32 : x * 32 + 32], second[:, x * 32 : x * 32 + 32]]
    out_ref[...] = jnp.maximum(jnp.concatenate(slots, 1), 0.0).astype(BF16)


def exchange(value, axes):
    return lax.all_to_all(value, axes, 0, 0, tiled=True)


def shape(*dims, dtype=BF16):
    return jax.ShapeDtypeStruct(dims, dtype)


def on_device(acts, dec_bias, enc_weight, enc_bias, dec_weight, dead_ids, tile_count, sample_rows):
    width, latents = enc_weight.shape
    depth, tokens = acts.shape
    tile = sample_rows.shape[2]
    slots = dead_ids.shape[1]

    counts = tile_count.T
    centered = (acts.astype(F32) - dec_bias[:, None]).astype(BF16)
    decoder = kernel_call(
        columns,
        shape(4, latents, width // 4),
        [ANY],
        0,
        56,
        [
            pltpu.VMEM((3, latents, width // 4), BF16),
            pltpu.SemaphoreType.DMA((3,)),
            pltpu.SemaphoreType.DMA((3,)),
        ],
        ANY,
    )(dec_weight)
    decoder = exchange(decoder, "y")
    by_z = lax.all_gather(centered, "z", axis=0, tiled=True)
    by_z = kernel_call(spread, shape(4, 16 * depth, tokens), [VM, ANY], 1 << 20, 3)(
        by_z, decoder
    )
    gathered = exchange(by_z, "y").reshape(width, tokens)

    features, by_token, stat = kernel_call(
        forward,
        (shape(4, tokens, latents), shape(tokens, width), shape(8, 128, dtype=F32)),
        [VM] * 5,
        2 * width * latents * tokens,
        8,
    )(counts, gathered, enc_weight, enc_bias.reshape(1, latents), dead_ids)
    features = exchange(features, "y")
    part = kernel_call(
        rebuild, shape(width // 4, tokens), [VM] * 3, 2 * width * latents * tokens, 6
    )(features, decoder, dec_weight)
    part = exchange(part.reshape(16, depth, tokens), "z")

    picks = kernel_call(
        residual,
        shape(16, depth + EXTRA, 4 * tile),
        [VM] * 4,
        2 * depth * tokens * 64 * tile,
        4,
    )(
        part,
        gathered.reshape(64, depth, tokens),
        sample_rows.transpose(1, 2, 0).reshape(tile, 64),
        stat,
    )
    picks = exchange(picks, "z")
    picks = kernel_call(relay, shape(16, tile, width // 4 + 128), [VM], 1 << 20, 2)(picks)
    picks = exchange(picks, ("y", "x"))
    rows = kernel_call(normalise, shape(4 * tile, width), [VM, VM], 1 << 21, 3)(counts, picks)
    other = lax.ppermute(rows, "core", [(0, 1), (1, 0)])
    new_enc, new_dec, token_loss, half = kernel_call(
        finish,
        (
            shape(tile, width),
            shape(tile, width),
            shape(1, tokens, dtype=F32),
            shape(tokens, 4 * tile, dtype=F32),
        ),
        [VM] * 4,
        tokens * slots * width,
        6,
    )(counts, picks, rows, by_token)
    reencoded = kernel_call(
        reencode, shape(tokens, slots), [VM] * 3, tokens * slots * width, 4
    )(other, by_token, half)
    return (new_enc, new_dec, reencoded, token_loss.reshape(tokens))


def solution(mesh):
    fine = Mesh(mesh.devices.reshape(16, 4, 4, 2), ("z", "y", "x", "core"))
    feat, tok = ("z", "y"), ("x", "core")
    in_specs = (
        P(feat, tok),
        P(feat),
        P(None, feat),
        P(feat),
        P(feat, None),
        P(feat, None),
        P(),
        P(None, tok, None),
    )
    out_specs = (P(feat + tok, None), P(feat + tok, None), P(tok, feat), P(tok))
    return jax.shard_map(
        on_device, mesh=fine, in_specs=in_specs, out_specs=out_specs, check_vma=False
    )
```

```python
import jax
import jax.numpy as jnp
from jax import lax
from jax.experimental import pallas as pl
from jax.experimental.pallas import tpu as pltpu
from jax.sharding import Mesh, PartitionSpec as P

ENC_GAIN = 0.2
EPSILON = 1e-06
F32 = jnp.float32
BF16 = jnp.bfloat16
VM = pl.BlockSpec(memory_space=pltpu.VMEM)
ANY = pl.BlockSpec(memory_space=pl.ANY)
EXTRA = 16
Z_ORDER = [(i + 8) % 16 for i in range(16)]


def kernel_call(body, out_shape, in_specs, flops, mib, scratch=(), out_specs=None):
    multi = isinstance(out_shape, (tuple, list))
    if out_specs is None:
        out_specs = [VM] * len(out_shape) if multi else VM
    return pl.pallas_call(
        body,
        out_shape=out_shape,
        in_specs=in_specs,
        out_specs=out_specs,
        scratch_shapes=list(scratch),
        compiler_params=pltpu.CompilerParams(vmem_limit_bytes=(mib + 4) << 20),
        cost_estimate=pl.CostEstimate(
            flops=flops, bytes_accessed=mib << 20, transcendentals=0
        ),
    )


def split3(v):
    hi = v.astype(BF16)
    rest = v - hi.astype(F32)
    mid = rest.astype(BF16)
    lo = (rest - mid.astype(F32)).astype(BF16)
    return hi, mid, lo


def spread(in_ref, after_ref, out_ref):
    for y in range(4):
        out_ref[y] = in_ref[...]


def own_counts(counts_ref):
    counts = counts_ref[...]
    feat = lax.axis_index("z") * 4 + lax.axis_index("y")
    shard = lax.broadcasted_iota(jnp.int32, counts.shape, 1)
    return jnp.sum(jnp.where(shard == feat, counts, 0), axis=1, keepdims=True)


def forward(counts_ref, g_ref, enc_ref, bias_ref, dead_ref, out_ref, t_ref, stat_ref):
    latents = enc_ref.shape[1]
    count = own_counts(counts_ref)
    row = lax.broadcasted_iota(jnp.int32, (latents, latents), 0)
    col = lax.broadcasted_iota(jnp.int32, (latents, latents), 1)
    slot = lax.broadcasted_iota(jnp.int32, (latents, 1), 0)
    limit = jnp.zeros((latents, 1), jnp.int32)
    for t in range(8):
        limit = jnp.where(slot // 32 == t, count[t : t + 1], limit)
    dead = jnp.sum(jnp.where(row == col, dead_ref[...], 0), axis=1, keepdims=True)
    dead = jnp.where(slot % 32 < limit, dead, -1)
    alive = 1.0 - jnp.max(jnp.where(dead == col, 1.0, 0.0), axis=0, keepdims=True)

    for z in range(16):
        for pair in range(2):
            y = 2 * pair
            both = jnp.concatenate(
                [
                    g_ref[pl.ds((y * 16 + z) * 64, 64), :],
                    g_ref[pl.ds(((y + 1) * 16 + z) * 64, 64), :],
                ],
                0,
            )
            t_ref[:, pl.ds(z * 256 + pair * 128, 128)] = both.T
    pre = jnp.dot(t_ref[...], enc_ref[...], preferred_element_type=F32) + bias_ref[...]
    feat = (jnp.maximum(pre, 0.0) * alive).astype(BF16)
    for y in range(4):
        out_ref[y] = feat
    total = jnp.zeros((8, latents), F32)
    for part in range(16):
        wide = enc_ref[pl.ds(part * 256, 256), :].astype(F32)
        total = total + jnp.sum((wide * wide).reshape(32, 8, latents), axis=0)
    norms = jnp.sqrt(jnp.sum(total, axis=0, keepdims=True))
    stat = jnp.sum(norms * alive, axis=1, keepdims=True)
    stat_ref[...] = jnp.broadcast_to(stat, stat_ref.shape)


def columns(in_ref, out_ref, held_ref, in_sems, out_sems):
    own = lax.axis_index("y")
    reads, writes = [], []
    for k in range(1, 4):
        y = lax.rem(own + k, 4)
        cols = pl.ds(pl.multiple_of(y * 1024, 1024), 1024)
        reads.append(
            pltpu.make_async_copy(in_ref.at[:, cols], held_ref.at[k - 1], in_sems.at[k - 1])
        )
        writes.append(
            pltpu.make_async_copy(held_ref.at[k - 1], out_ref.at[y], out_sems.at[k - 1])
        )
    for read in reads:
        read.start()
    for read, write in zip(reads, writes):
        read.wait()
        write.start()
    for write in writes:
        write.wait()


def rebuild(feat_ref, dec_ref, own_ref, out_ref):
    own = lax.axis_index("y")
    for block in range(4):
        cols = pl.ds(block * 256, 256)
        mine = pl.ds(pl.multiple_of(own * 1024 + block * 256, 256), 256)
        total = jnp.dot(feat_ref[own], own_ref[:, mine], preferred_element_type=F32)
        for k in range(1, 4):
            y = lax.rem(own + k, 4)
            total = total + jnp.dot(
                feat_ref[y], dec_ref[y, :, cols], preferred_element_type=F32
            )
        out_ref[pl.ds((block + 2) % 4 * 256, 256), :] = total.astype(BF16).T


def residual(part_ref, g_ref, sample_ref, stat_ref, out_ref):
    source = lax.axis_index("y") * 16 + lax.axis_index("z")
    own = g_ref[(source % 4) * 16 + source // 4]
    recon = part_ref[0].astype(F32)
    for z in range(1, 16):
        recon = recon + part_ref[z].astype(F32)
    error = own.astype(F32) - recon
    loss = jnp.sum(error * error, axis=0, keepdims=True)
    loss = jnp.concatenate([loss[:, :128], loss[:, 128:]], 0)
    stat = stat_ref[pl.ds(0, 2), :]
    pad = jnp.zeros((4, 128), F32)
    pieces = [split3(v) for v in (loss, stat)]
    extra = jnp.concatenate([p.astype(F32) for s in pieces for p in s] + [pad], 0).astype(BF16)
    error_b = error.astype(BF16)
    sample = sample_ref[...]
    shard = lax.broadcasted_iota(jnp.int32, sample.shape, 1)
    wide = jnp.concatenate([jnp.where(shard % 4 == y, sample, 0) for y in range(4)], 0)
    wide = jnp.concatenate([wide, jnp.zeros_like(wide)], 1).T
    token = lax.broadcasted_iota(jnp.int32, (error.shape[1], 128), 0)
    for z in range(16):
        wanted = jnp.sum(wide[z * 4 : z * 4 + 4], axis=0, keepdims=True)
        onehot = jnp.where(token == wanted, 1.0, 0.0).astype(BF16)
        picked = jnp.dot(error_b, onehot, preferred_element_type=F32)
        out_ref[(z + 8) % 16, pl.ds(0, 64), :] = picked.astype(BF16)
        out_ref[(z + 8) % 16, pl.ds(64, EXTRA), :] = extra


def relay(in_ref, out_ref):
    riders = in_ref[0, pl.ds(64, EXTRA), :].astype(F32)
    hi, mid, lo = riders[0:2], riders[2:4], riders[4:6]
    shi, smid, slo = riders[6:8], riders[8:10], riders[10:12]
    loss = hi + mid + lo
    stat = shi + smid + slo
    for z in range(1, 16):
        riders = in_ref[z, pl.ds(64, EXTRA), :].astype(F32)
        loss = loss + (riders[0:2] + riders[2:4] + riders[4:6])
        stat = stat + (riders[6:8] + riders[8:10] + riders[10:12])
    pieces = [p.astype(F32) for v in (loss, stat) for p in split3(v)]
    riders = jnp.concatenate(pieces + [jnp.zeros((20, 128), F32)], 0).astype(BF16)
    for pair in range(8):
        first = (2 * pair + 8) % 16
        both = jnp.concatenate(
            [in_ref[first, pl.ds(0, 64), :], in_ref[first + 1, pl.ds(0, 64), :]], 0
        ).T
        for y in range(4):
            for x in range(4):
                out_ref[y * 4 + x, :, pl.ds(pair * 128, 128)] = both[y * 32 : y * 32 + 32]
    for block in range(16):
        out_ref[block, :, pl.ds(1024, 128)] = riders


def tile_scale(in_ref, count, x):
    squares = jnp.zeros((32, 1024), F32)
    for y in range(4):
        rows = in_ref[y * 4 + x, :, pl.ds(0, 1024)].astype(F32)
        squares = squares + rows * rows
    squares = jnp.sum(squares, axis=1, keepdims=True)
    slot = lax.broadcasted_iota(jnp.int32, (32, 1), 0)
    return lax.rsqrt(squares + EPSILON) * jnp.where(slot < count, 1.0, 0.0)


def read_riders(counts_ref, in_ref, x):
    riders = jnp.zeros((EXTRA, 128), F32)
    for y in range(4):
        riders = riders + in_ref[y * 4 + x, pl.ds(0, EXTRA), pl.ds(1024, 128)].astype(F32)
    loss = riders[0:2] + riders[2:4] + riders[4:6]
    stat = riders[6:7] + riders[8:9] + riders[10:11]
    dead = jnp.sum(counts_ref[...].astype(F32), axis=0, keepdims=True)
    dead = jnp.sum(dead, axis=1, keepdims=True)
    gain = ENC_GAIN * (stat[:, 0:1] / (16384.0 - dead))
    return jnp.concatenate([loss[0:1], loss[1:2]], 1), gain


def tile_count(count, t):
    tile = lax.broadcasted_iota(jnp.int32, count.shape, 0)
    return jnp.sum(jnp.where(tile == t, count, 0), axis=0, keepdims=True)


def normalise(counts_ref, in_ref, rows_ref):
    core = lax.axis_index("core")
    count = own_counts(counts_ref)
    _, gain = read_riders(counts_ref, in_ref, 0)
    for x in range(4):
        scale = tile_scale(in_ref, tile_count(count, x * 2 + core), x)
        for y in range(4):
            unit = in_ref[y * 4 + x, :, pl.ds(0, 1024)].astype(F32) * scale
            rows_ref[pl.ds(x * 32, 32), pl.ds(y * 1024, 1024)] = (gain * unit).astype(BF16)


def finish(counts_ref, in_ref, rows_ref, t_ref, enc_ref, dec_ref, loss_ref, half_ref):
    x_own = lax.axis_index("x")
    core = lax.axis_index("core")
    count = own_counts(counts_ref)
    loss, _ = read_riders(counts_ref, in_ref, x_own)
    loss_ref[...] = loss * (1.0 / 4096.0)
    for x in range(4):

        @pl.when(x == x_own)
        def _(x=x):
            scale = tile_scale(in_ref, tile_count(count, x * 2 + core), x)
            for y in range(4):
                cols = pl.ds(y * 1024, 1024)
                unit = in_ref[y * 4 + x, :, pl.ds(0, 1024)].astype(F32) * scale
                dec_ref[:, cols] = unit.astype(BF16)
            enc_ref[...] = rows_ref[pl.ds(x * 32, 32), :]

    half_ref[...] = lax.dot_general(
        t_ref[...], rows_ref[...], (((1,), (1,)), ((), ())), preferred_element_type=F32
    )


def reencode(rows_ref, t_ref, half_ref, out_ref):
    core = lax.axis_index("core")
    other = lax.dot_general(
        t_ref[...], rows_ref[...], (((1,), (1,)), ((), ())), preferred_element_type=F32
    )
    own = half_ref[...]
    first = jnp.where(core == 0, own, other)
    second = jnp.where(core == 0, other, own)
    slots = []
    for x in range(4):
        slots += [first[:, x * 32 : x * 32 + 32], second[:, x * 32 : x * 32 + 32]]
    out_ref[...] = jnp.maximum(jnp.concatenate(slots, 1), 0.0).astype(BF16)


def exchange(value, axes):
    return lax.all_to_all(value, axes, 0, 0, tiled=True)


def exchange_z(value):
    return lax.all_to_all(value, "z", 0, 0, axis_index_groups=[Z_ORDER], tiled=True)


def shape(*dims, dtype=BF16):
    return jax.ShapeDtypeStruct(dims, dtype)


def on_device(acts, dec_bias, enc_weight, enc_bias, dec_weight, dead_ids, tile_count, sample_rows):
    width, latents = enc_weight.shape
    depth, tokens = acts.shape
    tile = sample_rows.shape[2]
    slots = dead_ids.shape[1]

    counts = tile_count.T
    centered = (acts.astype(F32) - dec_bias[:, None]).astype(BF16)
    decoder = kernel_call(
        columns,
        shape(4, latents, width // 4),
        [ANY],
        0,
        56,
        [
            pltpu.VMEM((3, latents, width // 4), BF16),
            pltpu.SemaphoreType.DMA((3,)),
            pltpu.SemaphoreType.DMA((3,)),
        ],
        ANY,
    )(dec_weight)
    decoder = exchange(decoder, "y")
    by_z = lax.all_gather(centered, "z", axis=0, tiled=True)
    by_z = kernel_call(spread, shape(4, 16 * depth, tokens), [VM, ANY], 1 << 20, 3)(
        by_z, decoder
    )
    gathered = exchange(by_z, "y").reshape(width, tokens)

    features, by_token, stat = kernel_call(
        forward,
        (shape(4, tokens, latents), shape(tokens, width), shape(8, 128, dtype=F32)),
        [VM] * 5,
        2 * width * latents * tokens,
        8,
    )(counts, gathered, enc_weight, enc_bias.reshape(1, latents), dead_ids)
    features = exchange(features, "y")
    part = kernel_call(
        rebuild, shape(width // 4, tokens), [VM] * 3, 2 * width * latents * tokens, 6
    )(features, decoder, dec_weight)
    part = exchange_z(part.reshape(16, depth, tokens))

    picks = kernel_call(
        residual,
        shape(16, depth + EXTRA, 4 * tile),
        [VM] * 4,
        2 * depth * tokens * 64 * tile,
        4,
    )(
        part,
        gathered.reshape(64, depth, tokens),
        sample_rows.transpose(1, 2, 0).reshape(tile, 64),
        stat,
    )
    picks = exchange_z(picks)
    picks = kernel_call(relay, shape(16, tile, width // 4 + 128), [VM], 1 << 20, 2)(picks)
    picks = exchange(picks, ("y", "x"))
    rows = kernel_call(normalise, shape(4 * tile, width), [VM, VM], 1 << 21, 3)(counts, picks)
    other = lax.ppermute(rows, "core", [(0, 1), (1, 0)])
    new_enc, new_dec, token_loss, half = kernel_call(
        finish,
        (
            shape(tile, width),
            shape(tile, width),
            shape(1, tokens, dtype=F32),
            shape(tokens, 4 * tile, dtype=F32),
        ),
        [VM] * 4,
        tokens * slots * width,
        6,
    )(counts, picks, rows, by_token)
    reencoded = kernel_call(
        reencode, shape(tokens, slots), [VM] * 3, tokens * slots * width, 4
    )(other, by_token, half)
    return (new_enc, new_dec, reencoded, token_loss.reshape(tokens))


def solution(mesh):
    fine = Mesh(mesh.devices.reshape(16, 4, 4, 2), ("z", "y", "x", "core"))
    feat, tok = ("z", "y"), ("x", "core")
    in_specs = (
        P(feat, tok),
        P(feat),
        P(None, feat),
        P(feat),
        P(feat, None),
        P(feat, None),
        P(),
        P(None, tok, None),
    )
    out_specs = (P(feat + tok, None), P(feat + tok, None), P(tok, feat), P(tok))
    return jax.shard_map(
        on_device, mesh=fine, in_specs=in_specs, out_specs=out_specs, check_vma=False
    )
```
